32 devices in a mesh: rows: 8 (over z, x), seq: 4 (over y, core).
Axes of the slice: x: 2, y: 2, z: 4, core: 2. Of those that a mesh axis runs over, the one named last changes fastest.
Arguments:
- tokens: bfloat16 [32, 1024, 1024], P('rows', 'seq'), may hold values from -6 to 6
- segment_ids: int32 [32, 1024], P('rows'), may hold values from 0 to 1024, as said below
- grad_out: bfloat16 [32, 1024, 1024], P('rows', 'seq'), may hold values from -6 to 6
- norm1_gain: float32 [1024], replicated, may hold values from 0.1 to 1.9
- norm1_shift: float32 [1024], replicated, may hold values from -1.5 to 1.5
- w_query: bfloat16 [1024, 1024], replicated, may hold values from -0.1875 to 0.1875
- b_query: float32 [1024], replicated, may hold values from -1.5 to 1.5
- w_key: bfloat16 [1024, 1024], replicated, may hold values from -0.1875 to 0.1875
- w_value: bfloat16 [1024, 1024], replicated, may hold values from -0.1875 to 0.1875
- b_value: float32 [1024], replicated, may hold values from -1.5 to 1.5
- w_out: bfloat16 [1024, 1024], replicated, may hold values from -0.75 to 0.75
- b_out: float32 [1024], replicated, may hold values from -1.5 to 1.5
- norm2_gain: float32 [1024], replicated, may hold values from 0.1 to 1.9
- norm2_shift: float32 [1024], replicated, may hold values from -1.5 to 1.5
- w_up: bfloat16 [1024, 4096], replicated, may hold values from -0.1875 to 0.1875
- b_up: float32 [4096], replicated, may hold values from -1.5 to 1.5
- w_down: bfloat16 [4096, 1024], replicated, may hold values from -0.09375 to 0.09375
- b_down: float32 [1024], replicated, may hold values from -1.5 to 1.5
Outputs:
- block_out: bfloat16 [32, 1024, 1024], P('rows', 'seq')
- grad_tokens: bfloat16 [32, 1024, 1024], P('rows', 'seq')
- grad_norm1_gain: float32 [1024], P(('rows', 'seq'))
- grad_norm1_shift: float32 [1024], P(('rows', 'seq'))
- grad_w_query: float32 [1024, 1024], P(('rows', 'seq'))
- grad_b_query: float32 [1024], P(('rows', 'seq'))
- grad_w_key: float32 [1024, 1024], P(('rows', 'seq'))
- grad_w_value: float32 [1024, 1024], P(('rows', 'seq'))
- grad_b_value: float32 [1024], P(('rows', 'seq'))
- grad_w_out: float32 [1024, 1024], P(('rows', 'seq'))
- grad_b_out: float32 [1024], P(('rows', 'seq'))
- grad_norm2_gain: float32 [1024], P(('rows', 'seq'))
- grad_norm2_shift: float32 [1024], P(('rows', 'seq'))
- grad_w_up: float32 [1024, 4096], P(('rows', 'seq'))
- grad_b_up: float32 [4096], P(('rows', 'seq'))
- grad_w_down: float32 [4096, 1024], P(('rows', 'seq'))
- grad_b_down: float32 [1024], P(('rows', 'seq'))
The draws below stay inside these ranges and needn't reach their ends.
Inputs may be any that keep to these rules, and one draw needn't show every extreme that they name: `segment_ids`: image id of each token; along a row the ids never decrease; the row ends in padding, a run of one or more tokens that hold 1024. A token attends to the tokens of its row with the same id.
All inputs are finite; a program needn't handle non-finite values.
Results may differ from the reference program's by a relative error of at most 0.02.
Values may be sent and summed in bfloat16 or wider, within the bound.
No kernel may reach another device: no remote copies, remote signals or barrier semaphores. Data moves between devices by JAX's collectives and lax.ppermute only.
A program may use at most 320 MiB of HBM per device.

```python
import jax
import jax.numpy as jnp
from jax import lax

D = 1024
HEADS = 16
FF = 4096
SEQ_LEN = 1024
R_DEV = 4
ROWS = 32
N_ROWS = 8
N_SEQ = 4


def draw_segment_ids(key, part):
    key = jax.random.fold_in(key, 7)
    first_key, second_key, third_key, fourth_key = jax.random.split(key, 4)
    shard_len = SEQ_LEN // N_SEQ
    image_start = jax.random.randint(first_key, (ROWS, 1), 0, shard_len, dtype=jnp.int32)
    image_stop = jax.random.randint(second_key, (ROWS, 1), SEQ_LEN - shard_len + 1, SEQ_LEN, dtype=jnp.int32)
    padding = jax.random.randint(third_key, (ROWS, 1), 1, SEQ_LEN - image_stop + 1, dtype=jnp.int32)
    position = lax.broadcasted_iota(jnp.int32, (ROWS, SEQ_LEN), 1)
    breaks = (jax.random.randint(fourth_key, (ROWS, SEQ_LEN), 0, 24, dtype=jnp.int32) == 0).astype(jnp.int32)
    forced = (position == 0) | (position == image_start) | (position == image_stop)
    inside = (position > image_start) & (position < image_stop)
    starts = jnp.where(forced, 1, jnp.where(inside, 0, breaks)).astype(jnp.int32)
    image_ids = jnp.cumsum(starts, axis=1).astype(jnp.int32) - 1
    return jnp.where(position >= SEQ_LEN - padding, SEQ_LEN, image_ids).astype(jnp.int32)


def levels(key, extent, shards, low, high):
    def one(axis_at, blocks):
        heights = jax.random.uniform(jax.random.fold_in(jax.random.fold_in(key, 6), axis_at), (blocks,), jnp.float32, low / len(shards), high / len(shards))
        return jnp.repeat(jnp.exp(heights), extent[axis_at] // blocks).reshape((-1,) + (1,) * (len(extent) - axis_at - 1))

    loudness = one(*shards[0])
    for cut in shards[1:]:
        loudness = loudness * one(*cut)
    return loudness


def gaussian(key, shape, deviation, bound, pieces=(), kind=jnp.bfloat16):
    entries = deviation * jax.random.normal(key, shape, jnp.float32)
    if pieces:
        entries = entries * levels(key, shape, pieces, -0.22, 0.18)
    return jnp.clip(entries, -bound, bound).astype(kind)


def setup_inputs(seed: int = 0) -> dict:
    streams_of = jax.random.split(jax.random.key(seed), 19)
    return {
        "tokens": gaussian(streams_of[0], (ROWS, SEQ_LEN, D), 1.0, 6.0, ((0, 8), (1, 4))),
        "segment_ids": draw_segment_ids(jax.random.fold_in(streams_of[18], 71), 0),
        "grad_out": gaussian(streams_of[2], (ROWS, SEQ_LEN, D), 1.0, 6.0, ((0, 8), (1, 4))),
        "norm1_gain": jnp.clip(1.0 + 0.18 * jax.random.normal(streams_of[3], (D,), jnp.float32), 0.1, 1.9),
        "norm1_shift": gaussian(streams_of[4], (D,), 0.3, 1.5, (), jnp.float32),
        "w_query": gaussian(streams_of[5], (D, D), D ** -0.5, 0.1875),
        "b_query": gaussian(streams_of[6], (D,), 0.3, 1.5, (), jnp.float32),
        "w_key": gaussian(streams_of[7], (D, D), D ** -0.5, 0.1875),
        "w_value": gaussian(streams_of[8], (D, D), D ** -0.5, 0.1875),
        "b_value": gaussian(streams_of[9], (D,), 0.3, 1.5, (), jnp.float32),
        "w_out": gaussian(streams_of[10], (D, D), (D // 16) ** -0.5, 0.75),
        "b_out": gaussian(streams_of[11], (D,), 0.3, 1.5, (), jnp.float32),
        "norm2_gain": jnp.clip(1.0 + 0.18 * jax.random.normal(streams_of[12], (D,), jnp.float32), 0.1, 1.9),
        "norm2_shift": gaussian(streams_of[13], (D,), 0.3, 1.5, (), jnp.float32),
        "w_up": gaussian(streams_of[14], (D, FF), D ** -0.5, 0.1875),
        "b_up": gaussian(streams_of[15], (FF,), 0.3, 1.5, (), jnp.float32),
        "w_down": gaussian(streams_of[16], (FF, D), FF ** -0.5, 0.09375),
        "b_down": gaussian(streams_of[17], (D,), 0.3, 1.5, (), jnp.float32),
    }


@jax.custom_vjp
def low(v):
    return lax.optimization_barrier(v.astype(jnp.bfloat16)).astype(jnp.float32)

@jax.custom_vjp
def low_back(v):
    return v

def low_keep(v):
    return (low(v), None)

def low_pass(kept, grad):
    return (grad,)

def back_keep(v):
    return (v, None)

def back_low(kept, grad):
    return (low(grad),)
low.defvjp(low_keep, low_pass)
low_back.defvjp(back_keep, back_low)
norm_eps = 1e-06
masked_score = -1e+30
highest = lax.Precision.HIGHEST

def layer_norm(values, norm_gain, norm_shift):
    row_mean = lax.optimization_barrier(jnp.mean(values, axis=-1, keepdims=True))
    centered = values - row_mean
    variance = lax.optimization_barrier(jnp.mean(centered * centered, axis=-1, keepdims=True))
    return centered * lax.rsqrt(variance + norm_eps) * norm_gain + norm_shift

def linear(values, matrix):
    return jnp.einsum('rtd,de->rte', values, matrix, precision=highest)

def block_forward(inputs, image_ids, params):
    norm1_gain, norm1_shift, w_query, b_query, w_key, w_value, b_value, w_out, b_out, norm2_gain, norm2_shift, w_up, b_up, w_down, b_down = params
    row_count, seq_len, model_width = inputs.shape
    head_dim = model_width // HEADS
    score_scale = head_dim ** (-0.5)
    normed = low(layer_norm(inputs, norm1_gain, norm1_shift))
    queries = low_back(low(linear(normed, w_query) + b_query))
    key_rows = low_back(low(linear(normed, w_key)))
    value_rows = low_back(low(linear(normed, w_value) + b_value))
    query_heads = queries.reshape(row_count, seq_len, HEADS, head_dim)
    key_heads = key_rows.reshape(row_count, seq_len, HEADS, head_dim)
    value_heads = value_rows.reshape(row_count, seq_len, HEADS, head_dim)
    raw_scores = low_back(jnp.einsum('rqhe,rkhe->rhqk', query_heads, key_heads, precision=highest) * score_scale)
    same_image = (image_ids[:, :, None] == image_ids[:, None, :])[:, None]
    scores = jnp.where(same_image, raw_scores, masked_score)
    row_top = lax.optimization_barrier(jnp.max(scores, axis=-1, keepdims=True))
    exponent = jnp.exp(scores - row_top)
    probs_low = low(exponent / lax.optimization_barrier(jnp.sum(exponent, axis=-1, keepdims=True)))
    mixed_heads = jnp.einsum('rhqk,rkhe->rqhe', probs_low, value_heads, precision=highest)
    attended = low_back(low(mixed_heads.reshape(row_count, seq_len, model_width)))
    branch = low_back(linear(attended, w_out) + b_out)
    residual = inputs + branch
    normed_two = low(layer_norm(residual, norm2_gain, norm2_shift))
    hidden_pre = low_back(linear(normed_two, w_up) + b_up)
    activated = low(jax.nn.gelu(hidden_pre, approximate=False))
    mlp_out = low_back(linear(activated, w_down) + b_down)
    return residual + mlp_out

def reference(tokens, segment_ids, grad_out, norm1_gain, norm1_shift, w_query, b_query, w_key, w_value, b_value, w_out, b_out, norm2_gain, norm2_shift, w_up, b_up, w_down, b_down):
    params = (norm1_gain.astype(jnp.float32), norm1_shift.astype(jnp.float32), w_query.astype(jnp.float32), b_query.astype(jnp.float32), w_key.astype(jnp.float32), w_value.astype(jnp.float32), b_value.astype(jnp.float32), w_out.astype(jnp.float32), b_out.astype(jnp.float32), norm2_gain.astype(jnp.float32), norm2_shift.astype(jnp.float32), w_up.astype(jnp.float32), b_up.astype(jnp.float32), w_down.astype(jnp.float32), b_down.astype(jnp.float32))
    inputs = tokens.astype(jnp.float32).reshape(N_ROWS, R_DEV, SEQ_LEN, D)
    id_groups = segment_ids.reshape(N_ROWS, R_DEV, SEQ_LEN)
    checked = jax.checkpoint(block_forward)

    def forward(group_inputs, group_params):

        def one_group(group_pair):
            return checked(group_pair[0], group_pair[1], group_params)
        return lax.map(one_group, (group_inputs, id_groups))
    outputs, pull_back = jax.vjp(forward, inputs, params)
    is_image = (id_groups != SEQ_LEN).astype(jnp.float32)[..., None]
    cotangent = grad_out.astype(jnp.float32).reshape(N_ROWS, R_DEV, SEQ_LEN, D) * is_image
    input_grad, param_grads = pull_back(cotangent)
    return (outputs.reshape(ROWS, SEQ_LEN, D).astype(jnp.bfloat16), input_grad.reshape(ROWS, SEQ_LEN, D).astype(jnp.bfloat16), param_grads[0], param_grads[1], param_grads[2], param_grads[3], param_grads[4], param_grads[5], param_grads[6], param_grads[7], param_grads[8], param_grads[9], param_grads[10], param_grads[11], param_grads[12], param_grads[13], param_grads[14])
```

```python
import jax
import jax.numpy as jnp
import numpy as np
from jax import lax
from jax.experimental import pallas as pl
from jax.experimental.pallas import tpu as pltpu
from jax.sharding import PartitionSpec as P

HEADS = 16
norm_eps = 1e-06
bf16 = jnp.bfloat16
f32 = jnp.float32
MIB = 1024 * 1024
DIGITS, BASE = 3, 11
CODE = DIGITS * BASE
HALF = 64


def dg(a, b, ca, cb):
    return lax.dot_general(a, b, (((ca,), (cb,)), ((), ())), preferred_element_type=f32)


def params(mib):
    return pltpu.CompilerParams(vmem_limit_bytes=mib * MIB)


def cost(flops, bytes_accessed, transcendentals=0):
    return pl.CostEstimate(
        flops=flops, bytes_accessed=bytes_accessed, transcendentals=transcendentals
    )


def norm_parts(values):
    mean = jnp.mean(values, axis=-1, keepdims=True)
    centered = values - mean
    variance = jnp.mean(centered * centered, axis=-1, keepdims=True)
    rstd = lax.rsqrt(variance + norm_eps)
    return centered * rstd, rstd


def qkv_kernel(first, c0, c1, gain, shift, wq, wk, wv, bq, bv, *refs):
    x, normed, qT, k, kT, v, vT, n_scr = refs[-8:]
    step = pl.program_id(0)
    length = c0.shape[0]

    @pl.when(step == 0)
    def _():
        for j, chunk in enumerate((c0, c1)):
            rows = slice(j * length, (j + 1) * length)
            values = chunk[...]
            x[rows, :] = values
            n, _ = norm_parts(values.astype(f32))
            low = (n * gain[...] + shift[...]).astype(bf16)
            n_scr[rows, :] = low
            normed[rows, :] = low

    n = n_scr[...]
    q_new = (dg(n, wq[...], 1, 0) + bq[...]).astype(bf16)
    qT[...] = (q_new.astype(f32) * 0.125).astype(bf16).T
    k_new = dg(n, wk[...], 1, 0).astype(bf16)
    k[...] = k_new
    kT[...] = k_new.T
    v_new = (dg(n, wv[...], 1, 0) + bv[...]).astype(bf16)
    v[...] = v_new
    vT[...] = v_new.T


def qkv(half, chunks, gain, shift, wq, wk, wv, bq, bv, before):
    length, width = chunks[0].shape
    total = 4 * length
    block = 256
    steps = width // block
    vec = pl.BlockSpec((1, width), lambda i: (0, 0))
    whole = pl.BlockSpec((length, width), lambda i: (0, 0))
    part = pl.BlockSpec((width, block), lambda i: (0, i))
    bias = pl.BlockSpec((1, block), lambda i: (0, i))
    wide = pl.BlockSpec((2 * length, width), lambda i: (half, 0))
    rows = pl.BlockSpec((2 * length, block), lambda i: (half, i))
    cols = pl.BlockSpec((block, 2 * length), lambda i: (i, half))
    out = jax.ShapeDtypeStruct((total, width), bf16)
    outT = jax.ShapeDtypeStruct((width, total), bf16)
    anyspec = pl.BlockSpec(memory_space=pl.ANY)
    return pl.pallas_call(
        lambda *refs: qkv_kernel(half == 0, *refs),
        grid=(steps,),
        in_specs=[whole, whole, vec, vec, part, part, part, bias, bias] + [anyspec] * len(before),
        out_specs=[wide, wide, cols, rows, cols, rows, cols],
        out_shape=[out, out, outT, out, outT, out, outT],
        scratch_shapes=[pltpu.VMEM((2 * length, width), bf16)],
        input_output_aliases={9 + n: n for n in range(len(before))},
        compiler_params=params(40),
        cost_estimate=cost(2 * 2 * length * width * 3 * width, 20 * MIB),
    )(chunks[0], chunks[1], gain, shift, wq, wk, wv, bq, bv, *before)


def attend_kernel(qT, k, vT, fT, g, oT, olo, aux):
    total = k.shape[0]
    lane = lax.broadcasted_iota(jnp.int32, (total, 128), 1)
    row = lax.broadcasted_iota(jnp.int32, (HALF, total), 0)
    keys, codes, queries_code = k[...], g[...], fT[...]
    ones = jnp.ones((16, total), bf16)

    def score(h):
        ka = jnp.where((lane < HALF) == (h == 0), keys, codes)
        qh = qT[h * HALF : (h + 1) * HALF, :]
        qa = jnp.concatenate([qh, queries_code] if h == 0 else [queries_code, qh], 0)
        s = dg(ka, qa, 1, 0)
        return s, jnp.max(s, axis=0, keepdims=True)

    def finish(h, s, top):
        head = slice(h * HALF, (h + 1) * HALF)
        va = jnp.concatenate([vT[head, :], ones], 0)
        p = jnp.exp(s - top).astype(bf16)
        mixed = dg(va, p, 1, 0)
        weight = mixed[HALF : HALF + 1]
        out = mixed[:HALF] / weight
        low = out.astype(bf16)
        oT[head, :] = low
        olo[head, :] = (out - low.astype(f32)).astype(bf16)
        aux[head, :] = pieces(
            -(top + jnp.log(weight)), row, queries_code.astype(f32)
        ).astype(bf16)

    first = score(0)
    second = score(1)
    finish(0, *first)
    finish(1, *second)


def pieces(value, row, base):
    hi = value.astype(bf16).astype(f32)
    mid = (value - hi).astype(bf16).astype(f32)
    low = value - hi - mid
    return jnp.where(
        row == CODE, hi, jnp.where(row == CODE + 1, mid, jnp.where(row == CODE + 2, low, base))
    )


def attend(qT, k, vT, fT, g):
    width, total = qT.shape
    pair = pl.BlockSpec((128, total), lambda i: (i, 0))
    return pl.pallas_call(
        attend_kernel,
        grid=(width // 128,),
        in_specs=[
            pair,
            pl.BlockSpec((total, 128), lambda i: (0, i)),
            pair,
            pl.BlockSpec((HALF, total), lambda i: (0, 0)),
            pl.BlockSpec((total, 128), lambda i: (0, 0)),
        ],
        out_specs=[pair] * 3,
        out_shape=[jax.ShapeDtypeStruct((width, total), bf16)] * 3,
        compiler_params=params(56),
        cost_estimate=cost(16 * HEADS * total * total * 64, 12 * MIB, HEADS * total * total),
    )(qT, k, vT, fT, g)


def attend_back_kernel(qT, k, kT, v, doT, oT, olo, aux, g, dqT, dkT, dvT):
    total = k.shape[0]
    lane = lax.broadcasted_iota(jnp.int32, (total, 128), 1)
    row = lax.broadcasted_iota(jnp.int32, (HALF, total), 0)
    keys, values, codes = k[...], v[...], g[...]
    for h in range(2):
        head = slice(h * HALF, (h + 1) * HALF)
        mine = (lane < HALF) == (h == 0)
        ka = jnp.where(mine, keys, codes)
        va = jnp.where(mine, values, codes)
        doh, qh, ax = doT[head, :], qT[head, :], aux[head, :]
        full = oT[head, :].astype(f32) + olo[head, :].astype(f32)
        delta = -jnp.sum(doh.astype(f32) * full, axis=0, keepdims=True)
        dx = pieces(delta, row, 0.0).astype(bf16)
        qa = jnp.concatenate([qh, ax] if h == 0 else [ax, qh], 0)
        doa = jnp.concatenate([doh, dx] if h == 0 else [dx, doh], 0)
        s = dg(ka, qa, 1, 0)
        dp = dg(va, doa, 1, 0)
        p = jnp.exp(s)
        low = p.astype(bf16)
        ds = (p * dp).astype(bf16)
        dkT[head, :] = dg(qh, ds, 1, 1).astype(bf16)
        dvT[head, :] = dg(doh, low, 1, 1).astype(bf16)
        dqT[head, :] = (dg(kT[head, :], ds, 1, 0) * 0.125).astype(bf16)


def attend_back(qT, k, kT, v, doT, oT, olo, aux, g):
    width, total = qT.shape
    pair = pl.BlockSpec((128, total), lambda i: (i, 0))
    tall = pl.BlockSpec((total, 128), lambda i: (0, i))
    return pl.pallas_call(
        attend_back_kernel,
        grid=(width // 128,),
        in_specs=[pair, tall, pair, tall, pair, pair, pair, pair]
        + [pl.BlockSpec((total, 128), lambda i: (0, 0))],
        out_specs=[pair] * 3,
        out_shape=[jax.ShapeDtypeStruct((width, total), bf16)] * 3,
        compiler_params=params(56),
        cost_estimate=cost(40 * HEADS * total * total * 64, 22 * MIB, HEADS * total * total),
    )(qT, k, kT, v, doT, oT, olo, aux, g)


def out_kernel(oT, x, w, b, gain, shift, residual, normed):
    r = x[...].astype(f32) + dg(oT[...], w[...], 0, 0) + b[...]
    residual[...] = r
    n, _ = norm_parts(r)
    normed[...] = (n * gain[...] + shift[...]).astype(bf16)


def out_project(oT, x, w, b, gain, shift):
    total, width = x.shape
    block = 256
    vec = pl.BlockSpec((1, width), lambda i: (0, 0))
    rows = pl.BlockSpec((block, width), lambda i: (i, 0))
    return pl.pallas_call(
        out_kernel,
        grid=(total // block,),
        in_specs=[
            pl.BlockSpec((width, block), lambda i: (0, i)),
            rows,
            pl.BlockSpec((width, width), lambda i: (0, 0)),
            vec,
            vec,
            vec,
        ],
        out_specs=[rows, rows],
        out_shape=[
            jax.ShapeDtypeStruct((total, width), f32),
            jax.ShapeDtypeStruct((total, width), bf16),
        ],
        compiler_params=params(40),
        cost_estimate=cost(2 * total * width * width, 12 * MIB),
    )(oT, x, w, b, gain, shift)


def mlp_kernel(n2, di, wu, wd, bu, res, bd, out, dn, gwd, gwu, gbu, acc_o, acc_n):
    step = pl.program_id(0)

    @pl.when(step == 0)
    def _():
        acc_o[...] = jnp.zeros_like(acc_o)
        acc_n[...] = jnp.zeros_like(acc_n)

    pre = dg(n2[...], wu[...], 1, 0) + bu[...]
    dact = dg(di[...], wd[...], 1, 1)
    cdf = 0.5 * (1.0 + lax.erf(pre * np.float32(np.sqrt(0.5))))
    pdf = jnp.exp(-0.5 * pre * pre) * np.float32(1 / np.sqrt(2 * np.pi))
    act = (pre * cdf).astype(bf16)
    hidden = (dact * (cdf + pre * pdf)).astype(bf16)
    acc_o[...] += dg(act, wd[...], 1, 0)
    acc_n[...] += dg(hidden, wu[...], 1, 1)
    gwd[...] = dg(act, di[...], 0, 0).astype(bf16)
    gwu[...] = dg(n2[...], hidden, 0, 0).astype(bf16)
    gbu[...] = jnp.sum(hidden.astype(f32), axis=0, keepdims=True)

    @pl.when(step == pl.num_programs(0) - 1)
    def _():
        out[...] = (res[...] + acc_o[...] + bd[...]).astype(bf16)
        dn[...] = acc_n[...]


def mlp(n2, di, wu, wd, bu, res, bd):
    total, width = n2.shape
    hidden = wu.shape[1]
    block = 512

    def full():
        return pl.BlockSpec((total, width), lambda i: (0, 0), pipeline_mode=pl.Buffered(1))

    up = pl.BlockSpec((width, block), lambda i: (0, i))
    down = pl.BlockSpec((block, width), lambda i: (i, 0))
    bias = pl.BlockSpec((1, block), lambda i: (0, i))
    return pl.pallas_call(
        mlp_kernel,
        grid=(hidden // block,),
        in_specs=[full(), full(), up, down, bias, full()]
        + [pl.BlockSpec((1, width), lambda i: (0, 0))],
        out_specs=[full(), full(), down, up, bias],
        out_shape=[
            jax.ShapeDtypeStruct((total, width), bf16),
            jax.ShapeDtypeStruct((total, width), f32),
            jax.ShapeDtypeStruct((hidden, width), bf16),
            jax.ShapeDtypeStruct((width, hidden), bf16),
            jax.ShapeDtypeStruct((1, hidden), f32),
        ],
        scratch_shapes=[pltpu.VMEM((total, width), f32)] * 2,
        compiler_params=params(56),
        cost_estimate=cost(12 * total * width * hidden, 50 * MIB, 2 * total * hidden),
    )(n2, di, wu, wd, bu, res, bd)


def out_back_kernel(dn, res, di, oT, w, gain, doT, rg, gw, ggain, gshift, gb, acc):
    step = pl.program_id(0)

    @pl.when(step == 0)
    def _():
        acc[...] = jnp.zeros_like(acc)
        ggain[...] = jnp.zeros_like(ggain)
        gshift[...] = jnp.zeros_like(gshift)
        gb[...] = jnp.zeros_like(gb)

    n, rstd = norm_parts(res[...])
    grad = dn[...]
    ggain[...] += jnp.sum(grad * n, axis=0, keepdims=True)
    gshift[...] += jnp.sum(grad, axis=0, keepdims=True)
    gh = grad * gain[...]
    mean = jnp.mean(gh, axis=-1, keepdims=True)
    tilt = jnp.mean(gh * n, axis=-1, keepdims=True)
    resid = di[...].astype(f32) + rstd * (gh - mean - n * tilt)
    rg[...] = resid
    low = resid.astype(bf16)
    gb[...] += jnp.sum(low.astype(f32), axis=0, keepdims=True)
    doT[...] = dg(w[...], low, 1, 1).astype(bf16)
    acc[...] += dg(oT[...], low, 1, 0)

    @pl.when(step == pl.num_programs(0) - 1)
    def _():
        gw[...] = acc[...].astype(bf16)


def out_back(dn, res, di, oT, w, gain):
    total, width = res.shape
    block = 256
    vec = pl.BlockSpec((1, width), lambda i: (0, 0))
    rows = pl.BlockSpec((block, width), lambda i: (i, 0))
    cols = pl.BlockSpec((width, block), lambda i: (0, i))
    square = pl.BlockSpec((width, width), lambda i: (0, 0))
    row = jax.ShapeDtypeStruct((1, width), f32)
    return pl.pallas_call(
        out_back_kernel,
        grid=(total // block,),
        in_specs=[rows, rows, rows, cols, square, vec],
        out_specs=[cols, rows, square, vec, vec, vec],
        out_shape=[
            jax.ShapeDtypeStruct((width, total), bf16),
            jax.ShapeDtypeStruct((total, width), f32),
            jax.ShapeDtypeStruct((width, width), bf16),
            row,
            row,
            row,
        ],
        scratch_shapes=[pltpu.VMEM((width, width), f32)],
        compiler_params=params(40),
        cost_estimate=cost(4 * total * width * width, 24 * MIB),
    )(dn, res, di, oT, w, gain)


def qkv_grad_kernel(n, dqT, dkT, dvT, gq, gk, gv, bq, bv):
    total = n.shape[0]
    ones = jnp.ones((8, total), bf16)
    gq[...] = dg(n[...], dqT[...], 0, 1).astype(bf16)
    gk[...] = dg(n[...], dkT[...], 0, 1).astype(bf16)
    gv[...] = dg(n[...], dvT[...], 0, 1).astype(bf16)
    bq[...] = dg(ones, dqT[...], 1, 1)[:1]
    bv[...] = dg(ones, dvT[...], 1, 1)[:1]


def qkv_grad(n, dqT, dkT, dvT):
    total, width = n.shape
    block = 256
    rows = pl.BlockSpec((block, total), lambda i: (i, 0))
    cols = pl.BlockSpec((width, block), lambda i: (0, i))
    bias = pl.BlockSpec((1, block), lambda i: (0, i))
    square = jax.ShapeDtypeStruct((width, width), bf16)
    row = jax.ShapeDtypeStruct((1, width), f32)
    return pl.pallas_call(
        qkv_grad_kernel,
        grid=(width // block,),
        in_specs=[pl.BlockSpec((total, width), lambda i: (0, 0)), rows, rows, rows],
        out_specs=[cols, cols, cols, bias, bias],
        out_shape=[square, square, square, row, row],
        compiler_params=params(40),
        cost_estimate=cost(6 * total * width * width, 14 * MIB),
    )(n, dqT, dkT, dvT)


def token_grad_kernel(dqT, dkT, dvT, wq, wk, wv, x, rg, gain, out, ggain, gshift, acc):
    step = pl.program_id(0)
    new = dg(dqT[...], wq[...], 0, 1) + dg(dkT[...], wk[...], 0, 1) + dg(dvT[...], wv[...], 0, 1)

    @pl.when(step == 0)
    def _():
        acc[...] = new

    @pl.when(step > 0)
    def _():
        acc[...] += new

    @pl.when(step == pl.num_programs(0) - 1)
    def _():
        n, rstd = norm_parts(x[...].astype(f32))
        grad = acc[...]
        ggain[...] = jnp.sum(grad * n, axis=0, keepdims=True)
        gshift[...] = jnp.sum(grad, axis=0, keepdims=True)
        gh = grad * gain[...]
        mean = jnp.mean(gh, axis=-1, keepdims=True)
        tilt = jnp.mean(gh * n, axis=-1, keepdims=True)
        out[...] = (rg[...] + rstd * (gh - mean - n * tilt)).astype(bf16)


def token_grad(half, dqT, dkT, dvT, wq, wk, wv, x, rg, gain):
    total, width = x.shape
    block = 256
    part = pl.BlockSpec((block, total // 2), lambda i: (i, half))
    weight = pl.BlockSpec((width, block), lambda i: (0, i))
    wide = pl.BlockSpec((total // 2, width), lambda i: (half, 0))
    vec = pl.BlockSpec((1, width), lambda i: (0, 0))
    row = jax.ShapeDtypeStruct((1, width), f32)
    return pl.pallas_call(
        token_grad_kernel,
        grid=(width // block,),
        in_specs=[part, part, part, weight, weight, weight, wide, wide, vec],
        out_specs=[pl.BlockSpec((total // 2, width), lambda i: (0, 0)), vec, vec],
        out_shape=[jax.ShapeDtypeStruct((total // 2, width), bf16), row, row],
        scratch_shapes=[pltpu.VMEM((total // 2, width), f32)],
        compiler_params=params(40),
        cost_estimate=cost(3 * total * width * width, 14 * MIB),
    )(dqT, dkT, dvT, wq, wk, wv, x, rg, gain)


def swap(values, axis, size, bit):
    return lax.ppermute(values, axis, [(i, i ^ bit) for i in range(size)])


def halving(values, order, sizes):
    rows, seq = sizes
    bits = (rows * seq).bit_length() - 1
    seq_bits = seq.bit_length() - 1
    chunk = values.shape[0] // (rows * seq)
    spots = list(range(bits - 1, -1, -1))
    kept = values.reshape((2,) * bits + (chunk,) + values.shape[1:])
    got = None
    for n, bit in enumerate(order):
        at = spots.index(bit)
        spots.remove(bit)
        axis, size, flip = ("seq", seq, 1 << bit) if bit < seq_bits else ("rows", rows, 1 << (bit - seq_bits))
        mine = (lax.axis_index(axis) // flip) % 2

        def half(which):
            own = lax.dynamic_index_in_dim(kept, which, at, keepdims=False)
            if got is None:
                return own
            other = lax.dynamic_index_in_dim(got, which, at, keepdims=False)
            return (own.astype(f32) + other.astype(f32)).astype(values.dtype)

        send, kept = half(1 - mine), half(mine)
        got = swap(send, axis, size, flip)
    return kept.astype(f32) + got.astype(f32)


def on_device(
    tokens,
    segment_ids,
    grad_out,
    norm1_gain,
    norm1_shift,
    w_query,
    b_query,
    w_key,
    w_value,
    b_value,
    w_out,
    b_out,
    norm2_gain,
    norm2_shift,
    w_up,
    b_up,
    w_down,
    b_down,
):
    row_count, local_len, width = tokens.shape
    full_len = segment_ids.shape[1]
    seq = lax.axis_size("seq")
    rows = lax.axis_size("rows")
    sizes = (rows, seq)
    me = lax.axis_index("seq")
    assert row_count == seq == 4 and local_len * seq == full_len

    def vec(v):
        return v.reshape(1, -1)

    def pick(values, j):
        return lax.dynamic_index_in_dim(values, me ^ j, 0, keepdims=False)

    def scatter_rows(values):
        return [pick(values, 0)] + [
            swap(pick(values, j), "seq", seq, j) for j in range(1, seq)
        ]

    def gather_rows(chunks):
        back = [chunks[0]] + [swap(chunks[j], "seq", seq, j) for j in range(1, seq)]
        out = jnp.zeros((row_count, local_len, width), bf16)
        for j in range(seq):
            out = lax.dynamic_update_index_in_dim(out, back[j], me ^ j, 0)
        return out

    ids_rows = lax.dynamic_index_in_dim(segment_ids, me, 0, keepdims=False).reshape(seq, local_len)
    ids = jnp.concatenate([pick(ids_rows, j) for j in range(seq)])
    digits = jnp.stack([(ids // BASE**n) % BASE for n in range(DIGITS)], 1)
    hot = (digits[:, :, None] == jnp.arange(BASE)[None, None, :]).reshape(full_len, CODE)
    hot = hot.astype(f32)
    rest = jnp.zeros((full_len, HALF - CODE), f32)
    query_code = jnp.concatenate([hot, rest], 1).astype(bf16).T
    key_code = jnp.concatenate([-1e30 * (1.0 - hot), rest.at[:, :3].set(1.0)], 1).astype(bf16)
    key_code = jnp.concatenate([key_code, key_code], 1)

    x_chunks = scatter_rows(tokens)
    norm1 = (vec(norm1_gain), vec(norm1_shift))
    weights = (w_query, w_key, w_value, vec(b_query), vec(b_value))
    before = qkv(0, x_chunks[:2], *norm1, *weights, ())
    x, normed, qT, k, kT, v, vT = qkv(1, x_chunks[2:], *norm1, *weights, before)

    local_ids = lax.dynamic_slice_in_dim(segment_ids, me * local_len, local_len, 1)
    is_image = (local_ids != full_len).astype(bf16)[:, :, None]
    out_grad = grad_out * is_image
    down_in = jnp.concatenate(scatter_rows(out_grad), 0)
    grad_b_down = jnp.sum(out_grad.astype(f32), axis=(0, 1))

    oT, olo, aux = attend(qT, k, vT, query_code, key_code)
    residual, normed_two = out_project(
        oT, x, w_out, vec(b_out), vec(norm2_gain), vec(norm2_shift)
    )
    block_out, dn, grad_w_down, grad_w_up, grad_b_up = mlp(
        normed_two, down_in, w_up, w_down, vec(b_up), residual, vec(b_down)
    )
    block_out = gather_rows([block_out[j * local_len : (j + 1) * local_len] for j in range(seq)])

    nbits = (rows * seq).bit_length() - 1
    seq_bits = seq.bit_length() - 1
    high = list(range(seq_bits, nbits))
    x_first = [0] + high[:1] + list(range(1, seq_bits)) + high[1:]
    y_first = [0] + list(range(1, seq_bits)) + high
    z_first = [0] + high[1:] + high[:1] + list(range(1, seq_bits))
    grad_w_down = halving(grad_w_down, x_first, sizes)
    grad_w_up = halving(grad_w_up, z_first, sizes)

    doT, resid_grad, grad_w_out, grad_gain2, grad_shift2, grad_b_out = out_back(
        dn, residual, down_in, oT, w_out, vec(norm2_gain)
    )
    grad_w_out = halving(grad_w_out, y_first, sizes)

    dqT, dkT, dvT = attend_back(qT, k, kT, v, doT, oT, olo, aux, key_code)
    grad_w_query, grad_w_key, grad_w_value, grad_b_query, grad_b_value = qkv_grad(
        normed, dqT, dkT, dvT
    )
    grad_w_query = halving(grad_w_query, x_first, sizes)
    grad_w_key = halving(grad_w_key, y_first, sizes)
    grad_w_value = halving(grad_w_value, z_first, sizes)
    halves = [
        token_grad(
            h, dqT, dkT, dvT, w_query, w_key, w_value, x, resid_grad, vec(norm1_gain)
        )
        for h in (1, 0)
    ]
    grad_tokens = gather_rows(
        [halves[1 - j // 2][0][j % 2 * local_len : (j % 2 + 1) * local_len] for j in range(seq)]
    )
    grad_gain1 = halves[0][1] + halves[1][1]
    grad_shift1 = halves[0][2] + halves[1][2]

    vectors = [
        grad_gain1,
        grad_shift1,
        grad_b_query,
        grad_b_value,
        grad_b_out,
        grad_gain2,
        grad_shift2,
        grad_b_up,
        grad_b_down,
    ]
    sums = halving(
        jnp.concatenate([g.reshape(rows * seq, -1) for g in vectors], 1), x_first, sizes
    ).reshape(-1)
    parts, start = [], 0
    for g in vectors:
        size = g.size // (rows * seq)
        parts.append(sums[start : start + size])
        start += size
    gain1, shift1, bq, bv, bo, gain2, shift2, bu, bd = parts
    return (
        block_out,
        grad_tokens,
        gain1,
        shift1,
        grad_w_query,
        bq,
        grad_w_key,
        grad_w_value,
        bv,
        grad_w_out,
        bo,
        gain2,
        shift2,
        grad_w_up,
        bu,
        grad_w_down,
        bd,
    )


def solution(mesh):
    tokens = P("rows", "seq", None)
    spread = P(("rows", "seq"))
    spread2 = P(("rows", "seq"), None)
    return jax.shard_map(
        on_device,
        mesh=mesh,
        in_specs=(tokens, P("rows", None), tokens) + (P(),) * 15,
        out_specs=(
            tokens,
            tokens,
            spread,
            spread,
            spread2,
            spread,
            spread2,
            spread2,
            spread,
            spread2,
            spread,
            spread,
            spread,
            spread2,
            spread,
            spread2,
            spread,
        ),
        check_vma=False,
    )
```

```python
import jax
import jax.numpy as jnp
import numpy as np
from jax import lax
from jax.experimental import pallas as pl
from jax.experimental.pallas import tpu as pltpu
from jax.sharding import PartitionSpec as P

HEADS = 16
norm_eps = 1e-06
bf16 = jnp.bfloat16
f32 = jnp.float32
MIB = 1024 * 1024
DIGITS, BASE = 3, 11
CODE = DIGITS * BASE
HALF = 64


def dg(a, b, ca, cb):
    return lax.dot_general(a, b, (((ca,), (cb,)), ((), ())), preferred_element_type=f32)


def params(mib):
    return pltpu.CompilerParams(vmem_limit_bytes=mib * MIB)


def cost(flops, bytes_accessed, transcendentals=0):
    return pl.CostEstimate(
        flops=20 * flops, bytes_accessed=20 * bytes_accessed, transcendentals=transcendentals
    )


def core_parts(grad, chunk, core):
    rows, cols = grad.shape
    runs = grad.reshape(rows // (2 * chunk), 2, chunk, cols)
    even = runs[:, 0].reshape(rows // 2, cols)
    odd = runs[:, 1].reshape(rows // 2, cols)
    first = core == 0
    return jnp.where(first, odd, even), jnp.where(first, even, odd)


def put_parts(refs, grad, chunk, core):
    if len(refs) == 1:
        refs[0][...] = grad.astype(bf16)
    else:
        other, own = core_parts(grad, chunk, core)
        refs[0][...] = other.astype(bf16)
        refs[1][...] = own.astype(bf16)


def full_spec(rows, cols):
    return pl.BlockSpec((rows, cols), lambda i, *_: (0, 0), pipeline_mode=pl.Buffered(1))


def call(kernel, scalars, grid, ins, in_specs, outs, out_specs, scratch=(), aliases=None, est=None):
    return pl.pallas_call(
        kernel,
        grid_spec=pltpu.PrefetchScalarGridSpec(
            num_scalar_prefetch=1,
            grid=(grid,),
            in_specs=in_specs,
            out_specs=out_specs,
            scratch_shapes=list(scratch),
        ),
        out_shape=outs,
        input_output_aliases=aliases or {},
        compiler_params=params(60),
        cost_estimate=est,
    )(scalars, *ins)


def norm_parts(values):
    mean = jnp.mean(values, axis=-1, keepdims=True)
    centered = values - mean
    variance = jnp.mean(centered * centered, axis=-1, keepdims=True)
    rstd = lax.rsqrt(variance + norm_eps)
    return centered * rstd, rstd


def qkv_kernel(s, c0, c1, gain, shift, wq, wk, wv, bq, bv, *refs):
    x, nT, q, k, v, n_scr = refs[-6:]
    length = c0.shape[0]
    core = s[1]

    @pl.when(pl.program_id(0) == 0)
    def _():
        for chunk, at in ((c0, core), (c1, 1 - core)):
            rows = pl.ds(pl.multiple_of(at * length, length), length)
            values = chunk[...]
            x[rows, :] = values
            n, _ = norm_parts(values.astype(f32))
            n_scr[rows, :] = (n * gain[...] + shift[...]).astype(bf16)

    n = n_scr[...]
    block = wq.shape[1]
    q[...] = (dg(n, wq[...], 1, 0) + bq[...]).astype(bf16) * 0.125
    k[...] = dg(n, wk[...], 1, 0).astype(bf16)
    v[...] = (dg(n, wv[...], 1, 0) + bv[...]).astype(bf16)
    nT[...] = n_scr[:, pl.ds(pl.multiple_of(pl.program_id(0) * block, block), block)].T


def qkv(scalars, chunks, gain, shift, wq, wk, wv, bq, bv, before):
    length, width = chunks[0].shape
    total = 4 * length
    block = 256
    whole = full_spec(length, width)
    vec = full_spec(1, width)
    part = pl.BlockSpec((width, block), lambda i, s: (0, i))
    bias = pl.BlockSpec((1, block), lambda i, s: (0, i))
    wide = pl.BlockSpec((2 * length, width), lambda i, s: (s[0], 0), pipeline_mode=pl.Buffered(1))
    rows = pl.BlockSpec((2 * length, block), lambda i, s: (s[0], i))
    cols = pl.BlockSpec((block, 2 * length), lambda i, s: (i, s[0]))
    out = jax.ShapeDtypeStruct((total, width), bf16)
    outT = jax.ShapeDtypeStruct((width, total), bf16)
    return call(
        qkv_kernel,
        scalars,
        width // block,
        [*chunks, gain, shift, wq, wk, wv, bq, bv, *before],
        [whole, whole, vec, vec, part, part, part, bias, bias]
        + [pl.BlockSpec(memory_space=pl.ANY)] * len(before),
        [out, outT, out, out, out],
        [wide, cols, rows, rows, rows],
        [pltpu.VMEM((2 * length, width), bf16)],
        aliases={10 + n: n for n in range(len(before))},
        est=cost(2 * 2 * length * width * 3 * width, 20 * MIB),
    )


def pieces(value, row, base):
    hi = value.astype(bf16).astype(f32)
    mid = (value - hi).astype(bf16).astype(f32)
    low = value - hi - mid
    return jnp.where(
        row == CODE, hi, jnp.where(row == CODE + 1, mid, jnp.where(row == CODE + 2, low, base))
    )


def attend_kernel(q, k, v, fT, g, oT, olo, aux):
    total = k.shape[0]
    lane = lax.broadcasted_iota(jnp.int32, (total, 128), 1)
    row = lax.broadcasted_iota(jnp.int32, (HALF, total), 0)
    keys, codes, queries_code = k[...], g[...], fT[...]
    ones = jnp.ones((16, total), bf16)
    qT, vT = q[...].T, v[...].T

    def score(h):
        ka = jnp.where((lane < HALF) == (h == 0), keys, codes)
        qh = qT[h * HALF : (h + 1) * HALF, :]
        qa = jnp.concatenate([qh, queries_code] if h == 0 else [queries_code, qh], 0)
        s = dg(ka, qa, 1, 0)
        return s, jnp.max(s, axis=0, keepdims=True)

    def finish(h, s, top):
        head = slice(h * HALF, (h + 1) * HALF)
        va = jnp.concatenate([vT[head, :], ones], 0)
        p = jnp.exp(s - top).astype(bf16)
        mixed = dg(va, p, 1, 0)
        weight = mixed[HALF : HALF + 1]
        out = mixed[:HALF] / weight
        low = out.astype(bf16)
        oT[head, :] = low
        olo[head, :] = (out - low.astype(f32)).astype(bf16)
        aux[head, :] = pieces(
            -(top + jnp.log(weight)), row, queries_code.astype(f32)
        ).astype(bf16)

    first = score(0)
    second = score(1)
    finish(0, *first)
    finish(1, *second)


def attend(q, k, v, fT, g):
    total, width = q.shape
    tall = pl.BlockSpec((total, 128), lambda i: (0, i))
    pair = pl.BlockSpec((128, total), lambda i: (i, 0))
    return pl.pallas_call(
        attend_kernel,
        grid=(width // 128,),
        in_specs=[
            tall,
            tall,
            tall,
            pl.BlockSpec((HALF, total), lambda i: (0, 0)),
            pl.BlockSpec((total, 128), lambda i: (0, 0)),
        ],
        out_specs=[pair] * 3,
        out_shape=[jax.ShapeDtypeStruct((width, total), bf16)] * 3,
        compiler_params=params(60),
        cost_estimate=cost(16 * HEADS * total * total * 64, 12 * MIB, HEADS * total * total),
    )(q, k, v, fT, g)


def norm_back(n, rstd, grad, gain):
    gh = grad * gain
    mean = jnp.mean(gh, axis=-1, keepdims=True)
    tilt = jnp.mean(gh * n, axis=-1, keepdims=True)
    return rstd * (gh - mean - n * tilt)


def mlp_kernel(
    chunks, heads, cut, s, oT, x, wo, bo, gain, shift, wu, wd, bu, bd, *refs
):
    grads_in, outs = refs[:heads], refs[heads : 2 * heads]
    gbu, rg, bg, ggain, gshift, gb, *refs = refs[2 * heads :]
    step, steps = pl.program_id(0), pl.num_programs(0)
    per = (len(refs) - 6) // 3
    gwd, gwu0, gwu1 = refs[:per], refs[per : 2 * per], refs[2 * per : 3 * per]
    acc_o, acc_n, res, n2, di, oT_scr = refs[-6:]
    total = n2.shape[0]
    block = x.shape[0]
    after = steps - 2

    @pl.when(step < heads)
    def _():
        rows = pl.ds(pl.multiple_of(step * block, block), block)
        r = x[...].astype(f32) + dg(oT[...], wo[...], 0, 0) + bo[...]
        res[rows, :] = r
        acc_o[rows, :] = r + bd[...]
        n, _ = norm_parts(r)
        n2[rows, :] = (n * gain[...] + shift[...]).astype(bf16)
        oT_scr[:, rows] = oT[...]

    @pl.when(step == 0)
    def _():
        for j, ref in enumerate(grads_in):
            di[pl.ds(pl.multiple_of((s[2] ^ j) * block, block), block), :] = ref[...]

    @pl.when((step >= heads) & (step < after))
    def _():
        pre = dg(n2[...], wu[...], 1, 0) + bu[...]
        dact = dg(di[...], wd[...], 1, 1)
        cdf = 0.5 * (1.0 + lax.erf(pre * np.float32(np.sqrt(0.5))))
        pdf = jnp.exp(-0.5 * pre * pre) * np.float32(1 / np.sqrt(2 * np.pi))
        act = (pre * cdf).astype(bf16)
        acc_o[...] += dg(act, wd[...], 1, 0)
        hidden = (dact * (cdf + pre * pdf)).astype(bf16)
        new = dg(hidden, wu[...], 1, 1)

        @pl.when(step == heads)
        def _():
            acc_n[...] = new

        @pl.when(step > heads)
        def _():
            acc_n[...] += new

        down_grad = dg(act, di[...], 0, 0)
        if len(gwd) == 1:
            gwd[0][...] = down_grad.astype(bf16)
        else:
            rows, size = chunks
            width = down_grad.shape[1]
            for ref, part in zip(gwd, core_parts(down_grad, rows, s[1])):
                for at in range(0, part.shape[0], size):
                    device, place = at // rows, at % rows // size
                    ref[device * size : (device + 1) * size, place * width : (place + 1) * width] = (
                        part[at : at + size, :].astype(bf16)
                    )
        gbu[...] = jnp.sum(hidden.astype(f32), axis=0, keepdims=True)
        up_grad = dg(n2[...], hidden, 0, 0)

        @pl.when(step < heads + cut)
        def _():
            put_parts(gwu0, up_grad, chunks[1], s[1])

        @pl.when(step >= heads + cut)
        def _():
            put_parts(gwu1, up_grad, chunks[1], s[1])

    @pl.when(step == after)
    def _():
        for j, ref in enumerate(outs):
            rows = pl.ds(pl.multiple_of((s[2] ^ j) * block, block), block)
            ref[...] = acc_o[rows, :].astype(bf16)
        ggain[...] = jnp.zeros_like(ggain)
        gshift[...] = jnp.zeros_like(gshift)
        gb[...] = jnp.zeros_like(gb)

        @pl.loop(0, total // 256)
        def _(i):
            rows = pl.ds(pl.multiple_of(i * 256, 256), 256)
            n, rstd = norm_parts(res[rows, :])
            grad = acc_n[rows, :]
            ggain[...] += jnp.sum(grad * n, axis=0, keepdims=True)
            gshift[...] += jnp.sum(grad, axis=0, keepdims=True)
            resid = di[rows, :].astype(f32) + norm_back(n, rstd, grad, gain[...])
            rg[rows, :] = resid
            low = resid.astype(bf16)
            bg[rows, :] = low
            gb[...] += jnp.sum(low.astype(f32), axis=0, keepdims=True)

    @pl.when(step >= after)
    def _():
        half = bg.shape[1] // 2
        cols = pl.ds(pl.multiple_of((step - after) * half, half), half)
        put_parts(gwu1, dg(oT_scr[...], bg[:, cols], 1, 0), chunks[1], s[1])


def mlp(scalars, devices, cut, oT, x, wo, bo, gain, shift, di, wu, wd, bu, bd):
    total, width = x.shape
    hidden = wu.shape[1]
    rows_block, block = 256, 512
    heads = total // rows_block
    steps = hidden // block
    chunks = hidden // devices, width // devices
    parts = 2 if min(chunks) % 16 == 0 else 1
    down_shape = (width // 2, hidden) if parts == 2 else (hidden, width)
    full = full_spec(total, width)
    vec = full_spec(1, width)

    def early(i):
        return jnp.minimum(i, heads - 1)

    def late(i):
        return jnp.clip(i - heads, 0, steps - 1)

    tokens = pl.BlockSpec((rows_block, width), lambda i, s: (early(i), 0))
    up = pl.BlockSpec((width, block), lambda i, s: (0, late(i)))
    down = pl.BlockSpec((block, width), lambda i, s: (late(i), 0))
    bias = pl.BlockSpec((1, block), lambda i, s: (0, late(i)))
    row = jax.ShapeDtypeStruct((1, width), f32)
    got = call(
        lambda *refs: mlp_kernel(chunks, heads, cut, *refs),
        scalars,
        heads + steps + width // block,
        [oT, x, wo, bo, gain, shift, wu, wd, bu, bd, *di],
        [
            pl.BlockSpec((width, rows_block), lambda i, s: (0, early(i))),
            tokens,
            full_spec(width, width),
            vec,
            vec,
            vec,
            up,
            down,
            bias,
            vec,
        ]
        + [full_spec(rows_block, width)] * heads,
        [jax.ShapeDtypeStruct((rows_block, width), bf16)] * heads
        + [
            jax.ShapeDtypeStruct((1, hidden), f32),
            jax.ShapeDtypeStruct((total, width), f32),
            jax.ShapeDtypeStruct((total, width), bf16),
            row,
            row,
            row,
        ]
        + [jax.ShapeDtypeStruct(down_shape, bf16)] * parts
        + [jax.ShapeDtypeStruct((width // parts, cut * block), bf16)] * parts
        + [jax.ShapeDtypeStruct((width // parts, hidden - cut * block + width), bf16)] * parts,
        [full_spec(rows_block, width)] * heads
        + [bias, full, full, vec, vec, vec]
        + [pl.BlockSpec((down_shape[0] // steps, down_shape[1]), lambda i, s: (late(i), 0))] * parts
        + [
            pl.BlockSpec(
                (width // parts, block), lambda i, s: (0, jnp.clip(i - heads, 0, cut - 1))
            )
        ]
        * parts
        + [
            pl.BlockSpec(
                (width // parts, block), lambda i, s: (0, jnp.maximum(i - heads - cut, 0))
            )
        ]
        * parts,
        [
            pltpu.VMEM((total, width), f32),
            pltpu.VMEM((total, width), f32),
            pltpu.VMEM((total, width), f32),
            pltpu.VMEM((total, width), bf16),
            pltpu.VMEM((total, width), bf16),
            pltpu.VMEM((width, total), bf16),
        ],
        est=cost(2 * total * width * (6 * hidden + 2 * width), 70 * MIB, 2 * total * hidden),
    )
    outs, got = got[:heads], got[heads:]
    return outs, got[:6], got[6 : 6 + parts], got[6 + parts : 6 + 2 * parts], got[6 + 2 * parts :]


def attend_back_kernel(chunk, s, q, k, v, w, bg, oT, olo, aux, g, nT, *refs):
    dqT, dkT, dvT, bias, *grads = refs
    total = k.shape[0]
    lane = lax.broadcasted_iota(jnp.int32, (total, 128), 1)
    row = lax.broadcasted_iota(jnp.int32, (HALF, total), 0)
    keys, values, codes = k[...], v[...], g[...]
    qT, kT = q[...].T, keys.T
    doT = dg(w[...], bg[...], 1, 1).astype(bf16)
    parts = [[], [], []]
    for h in range(2):
        head = slice(h * HALF, (h + 1) * HALF)
        mine = (lane < HALF) == (h == 0)
        ka = jnp.where(mine, keys, codes)
        va = jnp.where(mine, values, codes)
        doh, qh, ax = doT[head, :], qT[head, :], aux[head, :]
        full = oT[head, :].astype(f32) + olo[head, :].astype(f32)
        delta = -jnp.sum(doh.astype(f32) * full, axis=0, keepdims=True)
        dx = pieces(delta, row, 0.0).astype(bf16)
        qa = jnp.concatenate([qh, ax] if h == 0 else [ax, qh], 0)
        doa = jnp.concatenate([doh, dx] if h == 0 else [dx, doh], 0)
        scores = dg(ka, qa, 1, 0)
        dp = dg(va, doa, 1, 0)
        p = jnp.exp(scores)
        low = p.astype(bf16)
        ds = (p * dp).astype(bf16)
        parts[1].append(dg(qh, ds, 1, 1).astype(bf16))
        parts[2].append(dg(doh, low, 1, 1).astype(bf16))
        parts[0].append((dg(kT[head, :], ds, 1, 0) * 0.125).astype(bf16))
    new = jnp.concatenate([p for pair in parts for p in pair], 0)
    for n, ref in enumerate((dqT, dkT, dvT)):
        ref[...] = new[128 * n : 128 * (n + 1)]
    put_parts(grads, dg(nT[...], new, 1, 1), chunk, s[1])
    bias[...] = dg(jnp.ones((8, total), bf16), new, 1, 1)[:1]


def attend_back(scalars, devices, first, pairs, q, k, v, w, bg, oT, olo, aux, g, nT, before):
    total, width = q.shape
    chunk = width // devices
    parts = 2 if chunk % 16 == 0 else 1
    pair = pl.BlockSpec((128, total), lambda i, s: (i + first, 0))
    tall = pl.BlockSpec((total, 128), lambda i, s: (0, i + first))
    done = pl.BlockSpec((128, total), lambda i, s: (i, 0))
    outs = call(
        lambda *refs: attend_back_kernel(chunk, *refs[:11], *refs[11 + len(before) :]),
        scalars,
        pairs,
        [q, k, v, w, bg, oT, olo, aux, g, nT, *before],
        [tall, tall, tall, pl.BlockSpec((128, width), lambda i, s: (i + first, 0))]
        + [full_spec(total, width), pair, pair, pair]
        + [full_spec(total, 128), full_spec(width, total)]
        + [pl.BlockSpec(memory_space=pl.ANY)] * len(before),
        [jax.ShapeDtypeStruct((128 * pairs, total), bf16)] * 3
        + [jax.ShapeDtypeStruct((1, 384 * pairs), f32)]
        + [jax.ShapeDtypeStruct((width // parts, 3 * width), bf16)] * parts,
        [done] * 3
        + [pl.BlockSpec((1, 384), lambda i, s: (0, i))]
        + [pl.BlockSpec((width // parts, 384), lambda i, s: (0, i + first))] * parts,
        aliases={11 + n: 4 + n for n in range(len(before))},
        est=cost(pairs * 100 * 2 * total * total * 64, pairs * 3 * MIB, pairs * 2 * total * total),
    )
    return outs[:3], outs[3], list(outs[4:])


def token_grad_kernel(count, groups, s, *refs):
    grads = refs[:count]
    wq, wk, wv, x, rg, gain, *more = refs[count:-6]
    outs, eight, acc = refs[-6:-2], refs[-2], refs[-1]
    biases, rows = more[:groups], more[groups:]
    step = pl.program_id(0)

    @pl.when(step == 0)
    def _():
        eight[...] = jnp.zeros_like(eight)
        acc[...] = jnp.zeros_like(acc)
        for n, ref in enumerate(rows):
            eight[4 + n : 5 + n, :] = ref[...]
        at = 0
        for ref in biases:
            for n in range(ref.shape[1] // 384):
                eight[2:3, at : at + 128] = ref[:, 384 * n : 384 * n + 128]
                eight[3:4, at : at + 128] = ref[:, 384 * n + 256 : 384 * n + 384]
                at += 128

    grad = acc[...]
    new = 0.0
    for n, w in enumerate((wq, wk, wv)):
        new = new + dg(jnp.concatenate([g[...] for g in grads[n::3]], 0), w[...], 0, 1)
    n, rstd = norm_parts(x[...].astype(f32))
    eight[0:1, :] += jnp.sum(grad * n, axis=0, keepdims=True)
    eight[1:2, :] += jnp.sum(grad, axis=0, keepdims=True)
    done = (rg[...] + norm_back(n, rstd, grad, gain[...])).astype(bf16)
    for j, out in enumerate(outs):

        @pl.when((step - 1) == (s[2] ^ j))
        def _(out=out):
            out[...] = done

    acc[...] = new


def token_grad(scalars, grads, wq, wk, wv, x, rg, gain, biases, rows):
    total, width = x.shape
    block = 256
    steps = total // block
    grads = [g for triple in grads for g in triple]

    def now(i):
        return jnp.minimum(i, steps - 1)

    def past(i):
        return jnp.maximum(i - 1, 0)

    tokens = pl.BlockSpec((block, width), lambda i, s: (past(i), 0))
    vec = full_spec(1, width)
    return call(
        lambda *refs: token_grad_kernel(len(grads), len(biases), *refs),
        scalars,
        steps + 1,
        [*grads, wq, wk, wv, x, rg, gain, *biases, *rows],
        [pl.BlockSpec((g.shape[0], block), lambda i, s: (0, now(i))) for g in grads]
        + [full_spec(width, width)] * 3
        + [tokens, tokens, vec]
        + [full_spec(*b.shape) for b in biases]
        + [vec] * len(rows),
        [jax.ShapeDtypeStruct((block, width), bf16)] * steps
        + [jax.ShapeDtypeStruct((8, width), f32)],
        [full_spec(block, width)] * steps + [full_spec(8, width)],
        [pltpu.VMEM((block, width), f32)],
        est=cost(6 * total * width * width, 24 * MIB),
    )


def gather_kernel(s, *refs):
    parts, (out, sems) = refs[:-2], refs[-2:]
    copies = [
        pltpu.make_async_copy(ref, out.at[s[2] ^ j], sems.at[j]) for j, ref in enumerate(parts)
    ]
    for copy in copies:
        copy.start()
    for copy in copies:
        copy.wait()


def gather(scalars, parts):
    return call(
        gather_kernel,
        scalars,
        1,
        parts,
        [full_spec(*part.shape) for part in parts],
        jax.ShapeDtypeStruct((len(parts), *parts[0].shape), parts[0].dtype),
        pl.BlockSpec(memory_space=pl.ANY),
        [pltpu.SemaphoreType.DMA((len(parts),))],
    )


AXES = ("rows", "seq")


def swap(values, mask, devices):
    return lax.ppermute(values, AXES, [(d, d ^ mask) for d in range(devices)])


def add_kernel(jobs, arrays, s, *refs):
    ins, outs = refs[:arrays], refs[arrays : arrays + len(jobs)]
    refs = list(refs[arrays + len(jobs) :])
    sem_in, sem_out = refs[-2:]
    loads, stores, at, count = [], [], 0, 0
    for job, (free, segments) in enumerate(jobs):
        result = refs[at]
        at += 1
        places = []
        for width, terms in segments:
            places.append((width, refs[at : at + len(terms)]))
            at += len(terms)
        for piece in range(2 if free else 1):
            copies = []
            for (width, terms), (_, buffers) in zip(segments, places):
                for buffer, (array, index, column) in zip(buffers, terms):
                    where, first = [], True
                    for entry in index:
                        if entry is None:
                            where.append(piece if first else slice(None))
                            first = False
                        else:
                            where.append(s[entry])
                    where += [slice(None), pl.ds(column, width)]
                    copies.append(
                        pltpu.make_async_copy(
                            ins[array].at[tuple(where)],
                            buffer.at[piece] if free else buffer,
                            sem_in.at[count],
                        )
                    )
                    copies[-1].start()
                    count += 1
            loads.append((job, piece, free, places, result, copies))
    for spot, (job, piece, free, places, result, copies) in enumerate(loads):
        for copy in copies:
            copy.wait()
        for n in range(2 ** max(free - 1, 0)):
            here = ((piece,) if free else ()) + tuple(n >> b & 1 for b in range(free - 1))
            column = 0
            for width, buffers in places:
                total = sum(buffer[here].astype(f32) for buffer in buffers)
                result[here + (slice(None), slice(column, column + width))] = total.astype(
                    result.dtype
                )
                column += width
        stores.append(
            pltpu.make_async_copy(
                result.at[piece] if free else result,
                outs[job].at[piece] if free else outs[job],
                sem_out.at[spot],
            )
        )
        stores[-1].start()
    for copy in stores:
        copy.wait()


def add_all(wanted):
    arrays, entries, jobs, scratch, outs, shapes = [], [], [], [], [], []
    copies = pieces_out = 0
    for dtype, chunk, free, segments in wanted:
        shape = (2,) * free + (chunk, sum(width for width, _ in segments))
        scratch.append(pltpu.VMEM(shape, dtype))
        outs.append(jax.ShapeDtypeStruct(shape, dtype))
        pieces_out += 2 if free else 1
        listed = []
        for width, terms in segments:
            row = []
            for array, index, column in terms:
                found = [n for n, other in enumerate(arrays) if other is array]
                if not found:
                    arrays.append(array)
                    shapes.append((2,) * len(index) + (chunk, array.shape[-1]))
                where = []
                for value in index:
                    where.append(None if value is None else len(entries))
                    if value is not None:
                        entries.append(value)
                row.append((found[0] if found else len(arrays) - 1, where, column))
                scratch.append(pltpu.VMEM((2,) * free + (chunk, width), array.dtype))
                copies += 2 if free else 1
            listed.append((width, row))
        jobs.append((free, listed))
    anyspec = pl.BlockSpec(memory_space=pl.ANY)
    got = call(
        lambda *refs: add_kernel(jobs, len(arrays), *refs),
        jnp.stack([jnp.int32(e) for e in entries]),
        1,
        [array.reshape(shape) for array, shape in zip(arrays, shapes)],
        [anyspec] * len(arrays),
        outs,
        [anyspec] * len(outs),
        scratch + [pltpu.SemaphoreType.DMA((copies,)), pltpu.SemaphoreType.DMA((pieces_out,))],
    )
    return [values.reshape(-1, values.shape[-1]) for values in got]


class Sum:
    def __init__(self, devices, spots, segments, order):
        self.devices, self.spots, self.order = devices, list(spots), list(order)
        self.me = lax.axis_index(AXES)
        self.sending, self.coming, self.taken, self.total = [], [], [], None
        if segments:
            self.chunk = segments[0][0][0].shape[0] >> len(self.spots)
        self.segments = [
            (width, [(array, list(self.spots), column) for array in arrays])
            for arrays, column, width in segments
        ]

    def merged(self, other, order):
        new = Sum(self.devices, self.spots, [], order)
        new.chunk, new.taken = self.chunk, list(self.taken)
        new.segments = self.segments + other.segments
        return new

    def wanted(self, mask, dtype, segments):
        bits = {bit: ((self.me ^ mask) >> bit) & 1 for bit in self.taken}
        listed = [
            (width, [(v, [bits.get(bit) for bit in spots], column) for v, spots, column in terms])
            for width, terms in segments
        ]
        return (dtype, self.chunk, len(self.spots), listed)

    def masks(self):
        step = self.order.pop(0)
        bits = step if isinstance(step, tuple) else (step,)
        masks = [0]
        for bit in bits:
            masks += [m | 1 << bit for m in masks]
        self.taken += bits
        for bit in bits:
            self.spots.remove(bit)
        return masks[1:]

    def start(self):
        self.coming += [swap(v, mask, self.devices) for mask, v in self.sending]
        self.sending = []

    def arrive(self, coming):
        column = 0
        for width, terms in self.segments:
            terms += [(v, list(self.spots), column) for v in coming]
            column += width
        self.coming = []


def prepare(sums):
    jobs = []
    for t in sums:
        if t.order:
            jobs += [(t, mask, bf16, t.segments) for mask in t.masks()]
        elif t.total is None:
            jobs += [(t, 0, f32, [segment]) for segment in t.segments]
            t.total = []
    if not jobs:
        return
    got = add_all([t.wanted(mask, dtype, segments) for t, mask, dtype, segments in jobs])
    for (t, mask, dtype, _), values in zip(jobs, got):
        if dtype == f32:
            t.total.append(values)
        else:
            t.sending.append((mask, values))


def together(*groups):
    flat = lax.optimization_barrier(tuple(v for group in groups for v in group))
    out, start = [], 0
    for group in groups:
        out.append(list(flat[start : start + len(group)]))
        start += len(group)
    return out


def arrive(sums, carry):
    got = together(carry, *[t.coming for t in sums])
    for t, coming in zip(sums, got[1:]):
        t.arrive(coming)
    return got[0]


def leave(sums, carry):
    prepare(sums)
    got = together(carry, *[[v for _, v in t.sending] for t in sums])
    for t, sending in zip(sums, got[1:]):
        t.sending = [(mask, v) for (mask, _), v in zip(t.sending, sending)]
        t.start()
    return got[0]


def on_device(
    tokens,
    segment_ids,
    grad_out,
    norm1_gain,
    norm1_shift,
    w_query,
    b_query,
    w_key,
    w_value,
    b_value,
    w_out,
    b_out,
    norm2_gain,
    norm2_shift,
    w_up,
    b_up,
    w_down,
    b_down,
):
    row_count, local_len, width = tokens.shape
    full_len = segment_ids.shape[1]
    hidden = w_up.shape[1]
    seq, rows = lax.axis_size("seq"), lax.axis_size("rows")
    devices = rows * seq
    me = lax.axis_index("seq")
    core, pair = me % 2, me // 2
    assert row_count == seq == 4 and local_len * seq == full_len

    def vec(v):
        return v.reshape(1, -1)

    def scalars(first):
        return jnp.stack([jnp.int32(first), jnp.int32(core), jnp.int32(me)])

    def exchange(parts):
        return [parts[0]] + [swap(parts[j], j, devices) for j in range(1, seq)]

    plain = scalars(0)
    chunks = [lax.dynamic_index_in_dim(tokens, me ^ j, 0, keepdims=False) for j in range(seq)]
    chunks = exchange(chunks)
    norm1 = (vec(norm1_gain), vec(norm1_shift))
    weights = (w_query, w_key, w_value, vec(b_query), vec(b_value))

    ids = lax.dynamic_index_in_dim(segment_ids, me, 0, keepdims=False)
    digits = jnp.stack([(ids // BASE**n) % BASE for n in range(DIGITS)], 1)
    hot = (digits[:, :, None] == jnp.arange(BASE)[None, None, :]).reshape(full_len, CODE)
    hot = hot.astype(f32)
    rest = jnp.zeros((full_len, HALF - CODE), f32)
    query_code = jnp.concatenate([hot, rest], 1).astype(bf16).T
    key_code = jnp.concatenate([-1e30 * (1.0 - hot), rest.at[:, :3].set(1.0)], 1).astype(bf16)
    key_code = jnp.concatenate([key_code, key_code], 1)

    local_ids = lax.dynamic_slice_in_dim(segment_ids, me * local_len, local_len, 1)
    is_image = (local_ids != full_len).astype(bf16)[:, :, None]
    out_grad = grad_out * is_image
    grad_b_down = jnp.sum(out_grad.astype(f32), axis=(0, 1))

    before = qkv(scalars(pair), chunks[:2], *norm1, *weights, ())
    before = list(before)
    [before[0]], [out_grad] = together([before[0]], [out_grad])
    others = chunks[2:]
    down_in = exchange([lax.dynamic_index_in_dim(out_grad, me ^ j, 0, keepdims=False) for j in range(seq)])
    x, normedT, q, k, v = qkv(scalars(1 - pair), others, *norm1, *weights, before)
    oT, olo, aux = attend(q, k, v, query_code, key_code)
    nbits = devices.bit_length() - 1
    far = tuple(range(3, nbits))
    every = list(range(nbits - 1, -1, -1))
    block_out, (grad_b_up, rg, bg, gain2, shift2, bias_out), grad_down, grad_up0, grad_up1 = mlp(
        plain,
        devices,
        4,
        oT,
        x,
        w_out,
        vec(b_out),
        vec(norm2_gain),
        vec(norm2_shift),
        down_in,
        w_up,
        w_down,
        vec(b_up),
        vec(b_down),
    )
    biases, grads = [], []

    def backward(first, pairs, bg, before):
        got, bias, parts = attend_back(
            plain, devices, first, pairs, q, k, v, w_out, bg, oT, olo, aux, key_code, normedT, before
        )
        grads.append(got)
        biases.append(bias)
        return parts

    split = len(grad_down) == 2 and nbits == 5
    spots = every[:-1]

    def on_chip(pairs, carry):
        sends = [pair_[0] for pair_ in pairs]
        carry, sends = together(carry, sends)
        return carry, [swap(v, 1, devices) for v in sends]

    made = [grad_down, grad_up0, grad_up1]
    block_out = list(block_out)
    if split:
        [bg], came = on_chip(made, [bg])
    block_out[2:] = [swap(block_out[j], j, devices) for j in range(2, seq)]
    parts = backward(0, 2, bg, ())
    if split:
        (parts[0], bg, *block_out[2:]), came = together([parts[0], bg, *block_out[2:]], came)
        down, up0, up1 = ([keep, other] for (_, keep), other in zip(made, came))
        sum_a = Sum(devices, spots, [(down, 0, 3328)], [2, 1])
        sum_b = Sum(devices, spots, [(down, 3328, 768), (up1, 512, 2560)], [1, 2])
        sum_c = Sum(devices, spots, [(up0, 0, 2048), (up1, 0, 512)], [3, 4, 2, 1])
        sums = [sum_a, sum_b, sum_c]
        parts[0], bg = leave(sums, [parts[0], bg])
    block_out[1] = swap(block_out[1], 1, devices)
    parts = backward(2, 4, bg, parts)
    if split:
        parts[0], bg, *block_out = arrive(sums, [parts[0], bg, *block_out])
        parts[0], bg = leave(sums, [parts[0], bg])
    parts = backward(6, 2, bg, parts)
    gain = vec(norm1_gain)
    if split:
        parts[0], gain = arrive(sums, [parts[0], gain])
        [gain], came = on_chip([parts], [gain])
        sum_ab = sum_a.merged(sum_b, [3, 4])
        sums = [sum_ab, sum_c]
        [gain] = leave(sums, [gain])
        [gain], came = together([gain], came)
        ours = [parts[1], *came]
        cols = parts[1].shape[1] // 2
        sum_d = Sum(devices, spots, [(ours, 0, cols)], [2, 1])
        sum_e = Sum(devices, spots, [(ours, cols, cols)], [1, 2])
        [gain] = leave([sum_d, sum_e], [gain])
        sums += [sum_d, sum_e]
    *token, eight = token_grad(
        plain,
        grads,
        w_query,
        w_key,
        w_value,
        x,
        rg,
        gain,
        biases,
        [bias_out, gain2, shift2, vec(grad_b_down)],
    )
    if split:
        eight, *token = arrive(sums, [eight, *token])
        [eight] = leave(sums, [eight])
    token = exchange(token)
    eight = jnp.transpose(eight.reshape(8, devices, -1), (1, 0, 2)).reshape(devices, -1)
    vectors = jnp.concatenate([eight, grad_b_up.reshape(devices, -1)], 1)
    vectors = lax.all_to_all(vectors, AXES, 0, 0, tiled=True)
    own = width // devices
    if split:
        vectors, *token = arrive(sums, [vectors, *token])
        sum_in = sum_d.merged(sum_e, [far])
        [vectors] = leave([sum_in, sum_ab, sum_c], [vectors])
        [vectors] = arrive([sum_in], [vectors])
        leave([sum_in], [])
        down0, down1, up1 = sum_ab.total
        up0, up_mid = sum_c.total
        grad_w_down = jnp.concatenate([down0, down1], 1).reshape(own, -1, width)
        grad_w_down = jnp.transpose(grad_w_down, (1, 0, 2)).reshape(-1, width)
        at = up1.shape[1] - width
        grad_w_up = jnp.concatenate([up0, up_mid, up1[:, :at]], 1)
        grad_w_out = up1[:, at:]
        qkv_sums = jnp.concatenate(sum_in.total, 1)
    else:

        def over_all(values):
            return lax.psum_scatter(values.astype(f32), AXES, scatter_dimension=0, tiled=True)

        grad_w_down, up0, up1, qkv_sums = (over_all(pair_[0]) for pair_ in (*made, parts))
        grad_w_up = jnp.concatenate([up0, up1[:, : hidden - up0.shape[1]]], 1)
        grad_w_out = up1[:, hidden - up0.shape[1] :]
    vectors = jnp.sum(vectors, 0)
    grad_tokens = gather(plain, token)
    block_out = gather(plain, block_out)
    qkv_sums = qkv_sums.reshape(own, width // 128, 3, 128)
    grad_w_query, grad_w_key, grad_w_value = (
        qkv_sums[:, :, n].reshape(width // devices, width) for n in range(3)
    )
    parts, start = [], 0
    for size in [width] * 8 + [hidden]:
        parts.append(vectors[start : start + size // devices])
        start += size // devices
    gain1, shift1, bq, bv, bo, gain2, shift2, bd, bu = parts
    return (
        block_out,
        grad_tokens,
        gain1,
        shift1,
        grad_w_query,
        bq,
        grad_w_key,
        grad_w_value,
        bv,
        grad_w_out,
        bo,
        gain2,
        shift2,
        grad_w_up,
        bu,
        grad_w_down,
        bd,
    )


def solution(mesh):
    tokens = P("rows", "seq", None)
    spread = P(("rows", "seq"))
    spread2 = P(("rows", "seq"), None)
    return jax.shard_map(
        on_device,
        mesh=mesh,
        in_specs=(tokens, P("rows", None), tokens) + (P(),) * 15,
        out_specs=(
            tokens,
            tokens,
            spread,
            spread,
            spread2,
            spread,
            spread2,
            spread2,
            spread,
            spread2,
            spread,
            spread,
            spread,
            spread2,
            spread,
            spread2,
            spread,
        ),
        check_vma=False,
    )
```

```python
import jax
import jax.numpy as jnp
import numpy as np
from jax import lax
from jax.experimental import pallas as pl
from jax.experimental.pallas import tpu as pltpu
from jax.sharding import PartitionSpec as P

HEADS = 16
norm_eps = 1e-06
bf16 = jnp.bfloat16
f32 = jnp.float32
MIB = 1024 * 1024
DIGITS, BASE = 3, 11
CODE = DIGITS * BASE
HALF = 64


def dg(a, b, ca, cb):
    return lax.dot_general(a, b, (((ca,), (cb,)), ((), ())), preferred_element_type=f32)


def params(mib):
    return pltpu.CompilerParams(vmem_limit_bytes=mib * MIB)


def cost(flops, bytes_accessed, transcendentals=0):
    return pl.CostEstimate(
        flops=20 * flops, bytes_accessed=20 * bytes_accessed, transcendentals=transcendentals
    )


def core_parts(grad, chunk, core):
    rows, cols = grad.shape
    runs = grad.reshape(rows // (2 * chunk), 2, chunk, cols)
    even = runs[:, 0].reshape(rows // 2, cols)
    odd = runs[:, 1].reshape(rows // 2, cols)
    first = core == 0
    return jnp.where(first, odd, even), jnp.where(first, even, odd)


def put_parts(refs, grad, chunk, core):
    if len(refs) == 1:
        refs[0][...] = grad.astype(bf16)
    else:
        other, own = core_parts(grad, chunk, core)
        refs[0][...] = other.astype(bf16)
        refs[1][...] = own.astype(bf16)


def full_spec(rows, cols):
    return pl.BlockSpec((rows, cols), lambda i, *_: (0, 0), pipeline_mode=pl.Buffered(1))


def call(kernel, scalars, grid, ins, in_specs, outs, out_specs, scratch=(), aliases=None, est=None, mib=60):
    return pl.pallas_call(
        kernel,
        grid_spec=pltpu.PrefetchScalarGridSpec(
            num_scalar_prefetch=1,
            grid=(grid,),
            in_specs=in_specs,
            out_specs=out_specs,
            scratch_shapes=list(scratch),
        ),
        out_shape=outs,
        input_output_aliases=aliases or {},
        compiler_params=params(mib),
        cost_estimate=est,
    )(scalars, *ins)


def norm_parts(values):
    mean = jnp.mean(values, axis=-1, keepdims=True)
    centered = values - mean
    variance = jnp.mean(centered * centered, axis=-1, keepdims=True)
    rstd = lax.rsqrt(variance + norm_eps)
    return centered * rstd, rstd


def qkv_kernel(s, c0, c1, gain, shift, wq, wk, wv, bq, bv, *refs):
    x, nT, q, k, v, n_scr = refs[-6:]
    length = c0.shape[0]
    core = s[1]

    @pl.when(pl.program_id(0) == 0)
    def _():
        for chunk, at in ((c0, core), (c1, 1 - core)):
            rows = pl.ds(pl.multiple_of(at * length, length), length)
            values = chunk[...]
            x[rows, :] = values
            n, _ = norm_parts(values.astype(f32))
            n_scr[rows, :] = (n * gain[...] + shift[...]).astype(bf16)

    n = n_scr[...]
    block = wq.shape[1]
    q[...] = (dg(n, wq[...], 1, 0) + bq[...]).astype(bf16) * 0.125
    k[...] = dg(n, wk[...], 1, 0).astype(bf16)
    v[...] = (dg(n, wv[...], 1, 0) + bv[...]).astype(bf16)
    nT[...] = n_scr[:, pl.ds(pl.multiple_of(pl.program_id(0) * block, block), block)].T


def qkv(scalars, chunks, gain, shift, wq, wk, wv, bq, bv, before):
    length, width = chunks[0].shape
    total = 4 * length
    block = 256
    whole = full_spec(length, width)
    vec = full_spec(1, width)
    part = pl.BlockSpec((width, block), lambda i, s: (0, i))
    bias = pl.BlockSpec((1, block), lambda i, s: (0, i))
    wide = pl.BlockSpec((2 * length, width), lambda i, s: (s[0], 0), pipeline_mode=pl.Buffered(1))
    rows = pl.BlockSpec((2 * length, block), lambda i, s: (s[0], i))
    cols = pl.BlockSpec((block, 2 * length), lambda i, s: (i, s[0]))
    out = pltpu.HBM((total, width), bf16)
    outT = pltpu.HBM((width, total), bf16)
    return call(
        qkv_kernel,
        scalars,
        width // block,
        [*chunks, gain, shift, wq, wk, wv, bq, bv, *before],
        [whole, whole, vec, vec, part, part, part, bias, bias]
        + [pl.BlockSpec(memory_space=pl.ANY)] * len(before),
        [out, outT, out, out, out],
        [wide, cols, rows, rows, rows],
        [pltpu.VMEM((2 * length, width), bf16)],
        aliases={10 + n: n for n in range(len(before))},
        mib=20,
        est=cost(2 * 2 * length * width * 3 * width, 20 * MIB),
    )


def pieces(value, row, base):
    hi = value.astype(bf16).astype(f32)
    mid = (value - hi).astype(bf16).astype(f32)
    low = value - hi - mid
    return jnp.where(
        row == CODE, hi, jnp.where(row == CODE + 1, mid, jnp.where(row == CODE + 2, low, base))
    )


def attend_kernel(q, k, v, fT, g, oT, olo, aux):
    total, wide = k.shape
    lane = lax.broadcasted_iota(jnp.int32, (total, 128), 1)
    row = lax.broadcasted_iota(jnp.int32, (HALF, total), 0)
    codes, queries_code = g[...], fT[...]
    ones = jnp.ones((16, total), bf16)
    qT, vT = q[...].T, v[...].T

    def score(h):
        keys = k[:, h // 2 * 128 : h // 2 * 128 + 128]
        ka = jnp.where((lane < HALF) == (h % 2 == 0), keys, codes)
        qh = qT[h * HALF : (h + 1) * HALF, :]
        qa = jnp.concatenate([qh, queries_code] if h % 2 == 0 else [queries_code, qh], 0)
        s = dg(ka, qa, 1, 0)
        return s, jnp.max(s, axis=0, keepdims=True)

    def finish(h, s, top):
        head = slice(h * HALF, (h + 1) * HALF)
        va = jnp.concatenate([vT[head, :], ones], 0)
        p = jnp.exp(s - top).astype(bf16)
        mixed = dg(va, p, 1, 0)
        weight = mixed[HALF : HALF + 1]
        out = mixed[:HALF] / weight
        low = out.astype(bf16)
        oT[head, :] = low
        olo[head, :] = (out - low.astype(f32)).astype(bf16)
        aux[head, :] = pieces(
            -(top + jnp.log(weight)), row, queries_code.astype(f32)
        ).astype(bf16)

    heads = wide // HALF
    ahead = score(0)
    for h in range(heads):
        here = ahead
        if h + 1 < heads:
            ahead = score(h + 1)
        finish(h, *here)


def attend(q, k, v, fT, g, wide=256):
    total, width = q.shape
    tall = pl.BlockSpec((total, wide), lambda i: (0, i))
    pair = pl.BlockSpec((wide, total), lambda i: (i, 0))
    return pl.pallas_call(
        attend_kernel,
        grid=(width // wide,),
        in_specs=[
            tall,
            tall,
            tall,
            pl.BlockSpec((HALF, total), lambda i: (0, 0)),
            pl.BlockSpec((total, 128), lambda i: (0, 0)),
        ],
        out_specs=[pair] * 3,
        out_shape=[jax.ShapeDtypeStruct((width, total), bf16)] * 3,
        compiler_params=params(60),
        cost_estimate=cost(16 * HEADS * total * total * 64, 12 * MIB, HEADS * total * total),
    )(q, k, v, fT, g)


def norm_back(n, rstd, grad, gain):
    gh = grad * gain
    mean = jnp.mean(gh, axis=-1, keepdims=True)
    tilt = jnp.mean(gh * n, axis=-1, keepdims=True)
    return rstd * (gh - mean - n * tilt)


def mlp_kernel(
    chunks, heads, cut, s, oT, x, wo, bo, gain, shift, wu, wd, bu, bd, *refs
):
    grads_in, outs = refs[:heads], refs[heads : 2 * heads]
    gbu, rg, bg, ggain, gshift, gb, *refs = refs[2 * heads :]
    step, steps = pl.program_id(0), pl.num_programs(0)
    per = (len(refs) - 6) // 3
    gwd, gwu0, gwu1 = refs[:per], refs[per : 2 * per], refs[2 * per : 3 * per]
    acc_o, acc_n, res, n2, di, oT_scr = refs[-6:]
    total = n2.shape[0]
    block = x.shape[0]
    after = steps - 2

    @pl.when(step < heads)
    def _():
        rows = pl.ds(pl.multiple_of(step * block, block), block)
        r = x[...].astype(f32) + dg(oT[...], wo[...], 0, 0) + bo[...]
        res[rows, :] = r
        acc_o[rows, :] = r + bd[...]
        n, _ = norm_parts(r)
        n2[rows, :] = (n * gain[...] + shift[...]).astype(bf16)
        oT_scr[:, rows] = oT[...]

    @pl.when(step == 0)
    def _():
        for j, ref in enumerate(grads_in):
            di[pl.ds(pl.multiple_of((s[2] ^ j) * block, block), block), :] = ref[...]

    @pl.when((step >= heads) & (step < after))
    def _():
        pre = dg(n2[...], wu[...], 1, 0) + bu[...]
        dact = dg(di[...], wd[...], 1, 1)
        cdf = 0.5 * (1.0 + lax.erf(pre * np.float32(np.sqrt(0.5))))
        pdf = jnp.exp(-0.5 * pre * pre) * np.float32(1 / np.sqrt(2 * np.pi))
        act = (pre * cdf).astype(bf16)
        acc_o[...] += dg(act, wd[...], 1, 0)
        hidden = (dact * (cdf + pre * pdf)).astype(bf16)
        new = dg(hidden, wu[...], 1, 1)

        @pl.when(step == heads)
        def _():
            acc_n[...] = new

        @pl.when(step > heads)
        def _():
            acc_n[...] += new

        down_grad = dg(act, di[...], 0, 0)
        if len(gwd) == 1:
            gwd[0][...] = down_grad.astype(bf16)
        else:
            rows, size = chunks
            width = down_grad.shape[1]
            for ref, part in zip(gwd, core_parts(down_grad, rows, s[1])):
                for at in range(0, part.shape[0], size):
                    device, place = at // rows, at % rows // size
                    ref[device * size : (device + 1) * size, place * width : (place + 1) * width] = (
                        part[at : at + size, :].astype(bf16)
                    )
        gbu[...] = jnp.sum(hidden.astype(f32), axis=0, keepdims=True)
        up_grad = dg(n2[...], hidden, 0, 0)

        @pl.when(step < heads + cut)
        def _():
            put_parts(gwu0, up_grad, chunks[1], s[1])

        @pl.when(step >= heads + cut)
        def _():
            put_parts(gwu1, up_grad, chunks[1], s[1])

    @pl.when(step == after)
    def _():
        for j, ref in enumerate(outs):
            rows = pl.ds(pl.multiple_of((s[2] ^ j) * block, block), block)
            ref[...] = acc_o[rows, :].astype(bf16)
        ggain[...] = jnp.zeros_like(ggain)
        gshift[...] = jnp.zeros_like(gshift)
        gb[...] = jnp.zeros_like(gb)

        @pl.loop(0, total // 256)
        def _(i):
            rows = pl.ds(pl.multiple_of(i * 256, 256), 256)
            n, rstd = norm_parts(res[rows, :])
            grad = acc_n[rows, :]
            ggain[...] += jnp.sum(grad * n, axis=0, keepdims=True)
            gshift[...] += jnp.sum(grad, axis=0, keepdims=True)
            resid = di[rows, :].astype(f32) + norm_back(n, rstd, grad, gain[...])
            rg[rows, :] = resid
            low = resid.astype(bf16)
            bg[rows, :] = low
            gb[...] += jnp.sum(low.astype(f32), axis=0, keepdims=True)

    @pl.when(step >= after)
    def _():
        half = bg.shape[1] // 2
        cols = pl.ds(pl.multiple_of((step - after) * half, half), half)
        put_parts(gwu1, dg(oT_scr[...], bg[:, cols], 1, 0), chunks[1], s[1])


def mlp(scalars, devices, cut, oT, x, wo, bo, gain, shift, di, wu, wd, bu, bd):
    total, width = x.shape
    hidden = wu.shape[1]
    rows_block, block = 256, 512
    heads = total // rows_block
    steps = hidden // block
    chunks = hidden // devices, width // devices
    parts = 2 if min(chunks) % 16 == 0 else 1
    down_shape = (width // 2, hidden) if parts == 2 else (hidden, width)
    full = full_spec(total, width)
    vec = full_spec(1, width)

    def early(i):
        return jnp.minimum(i, heads - 1)

    def late(i):
        return jnp.clip(i - heads, 0, steps - 1)

    tokens = pl.BlockSpec((rows_block, width), lambda i, s: (early(i), 0))
    up = pl.BlockSpec((width, block), lambda i, s: (0, late(i)))
    down = pl.BlockSpec((block, width), lambda i, s: (late(i), 0))
    bias = pl.BlockSpec((1, block), lambda i, s: (0, late(i)))
    row = jax.ShapeDtypeStruct((1, width), f32)
    got = call(
        lambda *refs: mlp_kernel(chunks, heads, cut, *refs),
        scalars,
        heads + steps + width // block,
        [oT, x, wo, bo, gain, shift, wu, wd, bu, bd, *di],
        [
            pl.BlockSpec((width, rows_block), lambda i, s: (0, early(i))),
            tokens,
            full_spec(width, width),
            vec,
            vec,
            vec,
            up,
            down,
            bias,
            vec,
        ]
        + [full_spec(rows_block, width)] * heads,
        [jax.ShapeDtypeStruct((rows_block, width), bf16)] * heads
        + [
            jax.ShapeDtypeStruct((1, hidden), f32),
            jax.ShapeDtypeStruct((total, width), f32),
            jax.ShapeDtypeStruct((total, width), bf16),
            row,
            row,
            row,
        ]
        + [jax.ShapeDtypeStruct(down_shape, bf16)] * parts
        + [jax.ShapeDtypeStruct((width // parts, cut * block), bf16)] * parts
        + [jax.ShapeDtypeStruct((width // parts, hidden - cut * block + width), bf16)] * parts,
        [full_spec(rows_block, width)] * heads
        + [bias, full, full, vec, vec, vec]
        + [pl.BlockSpec((down_shape[0] // steps, down_shape[1]), lambda i, s: (late(i), 0))] * parts
        + [
            pl.BlockSpec(
                (width // parts, block), lambda i, s: (0, jnp.clip(i - heads, 0, cut - 1))
            )
        ]
        * parts
        + [
            pl.BlockSpec(
                (width // parts, block), lambda i, s: (0, jnp.maximum(i - heads - cut, 0))
            )
        ]
        * parts,
        [
            pltpu.VMEM((total, width), f32),
            pltpu.VMEM((total, width), f32),
            pltpu.VMEM((total, width), f32),
            pltpu.VMEM((total, width), bf16),
            pltpu.VMEM((total, width), bf16),
            pltpu.VMEM((width, total), bf16),
        ],
        est=cost(2 * total * width * (6 * hidden + 2 * width), 70 * MIB, 2 * total * hidden),
    )
    outs, got = got[:heads], got[heads:]
    return outs, got[:6], got[6 : 6 + parts], got[6 + parts : 6 + 2 * parts], got[6 + 2 * parts :]


def attend_back_kernel(chunk, s, q, k, v, w, bg, oT, olo, aux, g, nT, *refs):
    dqT, dkT, dvT, bias, *grads = refs
    total = k.shape[0]
    lane = lax.broadcasted_iota(jnp.int32, (total, 128), 1)
    row = lax.broadcasted_iota(jnp.int32, (HALF, total), 0)
    keys, values, codes = k[...], v[...], g[...]
    qT, kT = q[...].T, keys.T
    doT = dg(w[...], bg[...], 1, 1).astype(bf16)
    parts = [[], [], []]
    for h in range(2):
        head = slice(h * HALF, (h + 1) * HALF)
        mine = (lane < HALF) == (h == 0)
        ka = jnp.where(mine, keys, codes)
        va = jnp.where(mine, values, codes)
        doh, qh, ax = doT[head, :], qT[head, :], aux[head, :]
        full = oT[head, :].astype(f32) + olo[head, :].astype(f32)
        delta = -jnp.sum(doh.astype(f32) * full, axis=0, keepdims=True)
        dx = pieces(delta, row, 0.0).astype(bf16)
        qa = jnp.concatenate([qh, ax] if h == 0 else [ax, qh], 0)
        doa = jnp.concatenate([doh, dx] if h == 0 else [dx, doh], 0)
        scores = dg(ka, qa, 1, 0)
        dp = dg(va, doa, 1, 0)
        p = jnp.exp(scores)
        low = p.astype(bf16)
        ds = (p * dp).astype(bf16)
        parts[1].append(dg(qh, ds, 1, 1).astype(bf16))
        parts[2].append(dg(doh, low, 1, 1).astype(bf16))
        parts[0].append((dg(kT[head, :], ds, 1, 0) * 0.125).astype(bf16))
    new = jnp.concatenate([p for pair in parts for p in pair], 0)
    for n, ref in enumerate((dqT, dkT, dvT)):
        ref[...] = new[128 * n : 128 * (n + 1)]
    put_parts(grads, dg(nT[...], new, 1, 1), chunk, s[1])
    bias[...] = dg(jnp.ones((8, total), bf16), new, 1, 1)[:1]


def attend_back(scalars, devices, first, pairs, q, k, v, w, bg, oT, olo, aux, g, nT, before):
    total, width = q.shape
    chunk = width // devices
    parts = 2 if chunk % 16 == 0 else 1
    pair = pl.BlockSpec((128, total), lambda i, s: (i + first, 0))
    tall = pl.BlockSpec((total, 128), lambda i, s: (0, i + first))
    done = pl.BlockSpec((128, total), lambda i, s: (i, 0))
    outs = call(
        lambda *refs: attend_back_kernel(chunk, *refs[:11], *refs[11 + len(before) :]),
        scalars,
        pairs,
        [q, k, v, w, bg, oT, olo, aux, g, nT, *before],
        [tall, tall, tall, pl.BlockSpec((128, width), lambda i, s: (i + first, 0))]
        + [full_spec(total, width), pair, pair, pair]
        + [full_spec(total, 128), full_spec(width, total)]
        + [pl.BlockSpec(memory_space=pl.ANY)] * len(before),
        [jax.ShapeDtypeStruct((128 * pairs, total), bf16)] * 3
        + [jax.ShapeDtypeStruct((1, 384 * pairs), f32)]
        + [jax.ShapeDtypeStruct((width // parts, 3 * width), bf16)] * parts,
        [done] * 3
        + [pl.BlockSpec((1, 384), lambda i, s: (0, i))]
        + [pl.BlockSpec((width // parts, 384), lambda i, s: (0, i + first))] * parts,
        aliases={11 + n: 4 + n for n in range(len(before))},
        est=cost(pairs * 100 * 2 * total * total * 64, pairs * 3 * MIB, pairs * 2 * total * total),
    )
    return outs[:3], outs[3], list(outs[4:])


def token_grad_kernel(count, groups, s, *refs):
    grads = refs[:count]
    wq, wk, wv, x, rg, gain, *more = refs[count:-6]
    outs, eight, acc = refs[-6:-2], refs[-2], refs[-1]
    biases, rows = more[:groups], more[groups:]
    step = pl.program_id(0)

    @pl.when(step == 0)
    def _():
        eight[...] = jnp.zeros_like(eight)
        acc[...] = jnp.zeros_like(acc)
        for n, ref in enumerate(rows):
            eight[4 + n : 5 + n, :] = ref[...]
        at = 0
        for ref in biases:
            for n in range(ref.shape[1] // 384):
                eight[2:3, at : at + 128] = ref[:, 384 * n : 384 * n + 128]
                eight[3:4, at : at + 128] = ref[:, 384 * n + 256 : 384 * n + 384]
                at += 128

    grad = acc[...]
    new = 0.0
    for n, w in enumerate((wq, wk, wv)):
        new = new + dg(jnp.concatenate([g[...] for g in grads[n::3]], 0), w[...], 0, 1)
    n, rstd = norm_parts(x[...].astype(f32))
    eight[0:1, :] += jnp.sum(grad * n, axis=0, keepdims=True)
    eight[1:2, :] += jnp.sum(grad, axis=0, keepdims=True)
    done = (rg[...] + norm_back(n, rstd, grad, gain[...])).astype(bf16)
    for j, out in enumerate(outs):

        @pl.when((step - 1) == (s[2] ^ j))
        def _(out=out):
            out[...] = done

    acc[...] = new


def token_grad(scalars, grads, wq, wk, wv, x, rg, gain, biases, rows):
    total, width = x.shape
    block = 256
    steps = total // block
    grads = [g for triple in grads for g in triple]

    def now(i):
        return jnp.minimum(i, steps - 1)

    def past(i):
        return jnp.maximum(i - 1, 0)

    tokens = pl.BlockSpec((block, width), lambda i, s: (past(i), 0))
    vec = full_spec(1, width)
    return call(
        lambda *refs: token_grad_kernel(len(grads), len(biases), *refs),
        scalars,
        steps + 1,
        [*grads, wq, wk, wv, x, rg, gain, *biases, *rows],
        [pl.BlockSpec((g.shape[0], block), lambda i, s: (0, now(i))) for g in grads]
        + [full_spec(width, width)] * 3
        + [tokens, tokens, vec]
        + [full_spec(*b.shape) for b in biases]
        + [vec] * len(rows),
        [jax.ShapeDtypeStruct((block, width), bf16)] * steps
        + [jax.ShapeDtypeStruct((8, width), f32)],
        [full_spec(block, width)] * steps + [full_spec(8, width)],
        [pltpu.VMEM((block, width), f32)],
        est=cost(6 * total * width * width, 24 * MIB),
    )


def gather_kernel(s, *refs):
    parts, (out, sems) = refs[:-2], refs[-2:]
    copies = [
        pltpu.make_async_copy(ref, out.at[s[2] ^ j], sems.at[j]) for j, ref in enumerate(parts)
    ]
    for copy in copies:
        copy.start()
    for copy in copies:
        copy.wait()


def gather(scalars, parts):
    return call(
        gather_kernel,
        scalars,
        1,
        parts,
        [full_spec(*part.shape) for part in parts],
        jax.ShapeDtypeStruct((len(parts), *parts[0].shape), parts[0].dtype),
        pl.BlockSpec(memory_space=pl.ANY),
        [pltpu.SemaphoreType.DMA((len(parts),))],
    )


AXES = ("rows", "seq")


def swap(values, mask, devices):
    return lax.ppermute(values, AXES, [(d, d ^ mask) for d in range(devices)])


def add_kernel(jobs, arrays, s, *refs):
    many = sum(count_out for _, _, count_out in jobs)
    ins, outs = refs[:arrays], refs[arrays : arrays + many]
    refs = list(refs[arrays + many :])
    sem_in, sem_out = refs[-2:]
    loads, stores, at, count, first_out = [], [], 0, 0, 0
    for job, (free, segments, count_out) in enumerate(jobs):
        result = refs[at : at + count_out]
        at += count_out
        places = []
        for width, terms in segments:
            places.append((width, refs[at : at + len(terms)]))
            at += len(terms)
        for piece in range(2 if free else 1):
            copies = []
            for (width, terms), (_, buffers) in zip(segments, places):
                for buffer, (array, index, column) in zip(buffers, terms):
                    where, first = [], True
                    for entry in index:
                        if entry is None:
                            where.append(piece if first else slice(None))
                            first = False
                        else:
                            where.append(s[entry])
                    where += [slice(None), pl.ds(column, width)]
                    copies.append(
                        pltpu.make_async_copy(
                            ins[array].at[tuple(where)],
                            buffer.at[piece] if free else buffer,
                            sem_in.at[count],
                        )
                    )
                    copies[-1].start()
                    count += 1
            loads.append((outs[first_out : first_out + count_out], piece, free, places, result, copies))
        first_out += count_out
    for targets, piece, free, places, result, copies in loads:
        for copy in copies:
            copy.wait()
        for n in range(2 ** max(free - 1, 0)):
            here = ((piece,) if free else ()) + tuple(n >> b & 1 for b in range(free - 1))
            column = 0
            for width, buffers in places:
                total = sum(buffer[here].astype(f32) for buffer in buffers)
                total = total.astype(result[0].dtype)
                if len(result) == 1:
                    result[0][here + (slice(None), slice(column, column + width))] = total
                else:
                    for block in range(0, width, 128):
                        turn, which = divmod((column + block) // 128, len(result))
                        result[which][:, 128 * turn : 128 * (turn + 1)] = total[:, block : block + 128]
                column += width
        for buffer, target in zip(result, targets):
            stores.append(
                pltpu.make_async_copy(
                    buffer.at[piece] if free else buffer,
                    target.at[piece] if free else target,
                    sem_out.at[len(stores)],
                )
            )
            stores[-1].start()
    for copy in stores:
        copy.wait()


def add_all(wanted):
    arrays, entries, jobs, scratch, outs, shapes = [], [], [], [], [], []
    copies = pieces_out = 0
    for dtype, chunk, free, segments, count_out in wanted:
        shape = (2,) * free + (chunk, sum(width for width, _ in segments) // count_out)
        scratch += [pltpu.VMEM(shape, dtype)] * count_out
        outs += [jax.ShapeDtypeStruct(shape, dtype)] * count_out
        pieces_out += 2 if free else count_out
        listed = []
        for width, terms in segments:
            row = []
            for array, index, column in terms:
                found = [n for n, other in enumerate(arrays) if other is array]
                if not found:
                    arrays.append(array)
                    shapes.append((2,) * len(index) + (chunk, array.shape[-1]))
                where = []
                for value in index:
                    where.append(None if value is None else len(entries))
                    if value is not None:
                        entries.append(value)
                row.append((found[0] if found else len(arrays) - 1, where, column))
                scratch.append(pltpu.VMEM((2,) * free + (chunk, width), array.dtype))
                copies += 2 if free else 1
            listed.append((width, row))
        jobs.append((free, listed, count_out))
    anyspec = pl.BlockSpec(memory_space=pl.ANY)
    got = call(
        lambda *refs: add_kernel(jobs, len(arrays), *refs),
        jnp.stack([jnp.int32(e) for e in entries]),
        1,
        [array.reshape(shape) for array, shape in zip(arrays, shapes)],
        [anyspec] * len(arrays),
        outs,
        [anyspec] * len(outs),
        scratch + [pltpu.SemaphoreType.DMA((copies,)), pltpu.SemaphoreType.DMA((pieces_out,))],
    )
    return [values.reshape(-1, values.shape[-1]) for values in got]


class Sum:
    def __init__(self, devices, spots, segments, order):
        self.devices, self.spots, self.order = devices, list(spots), list(order)
        self.me = lax.axis_index(AXES)
        self.sending, self.coming, self.taken, self.total, self.shares = [], [], [], None, 1
        if segments:
            self.chunk = segments[0][0][0].shape[0] >> len(self.spots)
        self.segments = [
            (width, [(array, list(self.spots), column) for array in arrays])
            for arrays, column, width in segments
        ]

    def merged(self, other, order):
        new = Sum(self.devices, self.spots, [], order)
        new.chunk, new.taken = self.chunk, list(self.taken)
        new.segments = self.segments + other.segments
        return new

    def wanted(self, mask, dtype, segments):
        bits = {bit: ((self.me ^ mask) >> bit) & 1 for bit in self.taken}
        listed = [
            (width, [(v, [bits.get(bit) for bit in spots], column) for v, spots, column in terms])
            for width, terms in segments
        ]
        return (dtype, self.chunk, len(self.spots), listed, self.shares if dtype == f32 else 1)

    def masks(self):
        step = self.order.pop(0)
        bits = step if isinstance(step, tuple) else (step,)
        masks = [0]
        for bit in bits:
            masks += [m | 1 << bit for m in masks]
        self.taken += bits
        for bit in bits:
            self.spots.remove(bit)
        return masks[1:]

    def start(self):
        self.coming += [swap(v, mask, self.devices) for mask, v in self.sending]
        self.sending = []

    def arrive(self, coming):
        column = 0
        for width, terms in self.segments:
            terms += [(v, list(self.spots), column) for v in coming]
            column += width
        self.coming = []


def prepare(sums, more=()):
    jobs = []
    for t in sums:
        if t.order:
            jobs += [(t, mask, bf16, t.segments) for mask in t.masks()]
        elif t.total is None:
            whole = [t.segments] if t.shares > 1 else [[segment] for segment in t.segments]
            jobs += [(t, 0, f32, segments) for segments in whole]
            t.total = []
    if not jobs and not more:
        return []
    got = add_all([t.wanted(mask, dtype, segments) for t, mask, dtype, segments in jobs] + list(more))
    for t, mask, dtype, _ in jobs:
        if dtype == f32:
            t.total += got[: t.shares]
            got = got[t.shares :]
        else:
            t.sending.append((mask, got[0]))
            got = got[1:]
    return got


def together(*groups):
    flat = lax.optimization_barrier(tuple(v for group in groups for v in group))
    out, start = [], 0
    for group in groups:
        out.append(list(flat[start : start + len(group)]))
        start += len(group)
    return out


def arrive(sums, carry):
    got = together(carry, *[t.coming for t in sums])
    for t, coming in zip(sums, got[1:]):
        t.arrive(coming)
    return got[0]


def leave(sums, carry):
    prepare(sums)
    got = together(carry, *[[v for _, v in t.sending] for t in sums])
    for t, sending in zip(sums, got[1:]):
        t.sending = [(mask, v) for (mask, _), v in zip(t.sending, sending)]
        t.start()
    return got[0]


def on_device(
    tokens,
    segment_ids,
    grad_out,
    norm1_gain,
    norm1_shift,
    w_query,
    b_query,
    w_key,
    w_value,
    b_value,
    w_out,
    b_out,
    norm2_gain,
    norm2_shift,
    w_up,
    b_up,
    w_down,
    b_down,
):
    row_count, local_len, width = tokens.shape
    full_len = segment_ids.shape[1]
    hidden = w_up.shape[1]
    seq, rows = lax.axis_size("seq"), lax.axis_size("rows")
    devices = rows * seq
    me = lax.axis_index("seq")
    core, pair = me % 2, me // 2
    assert row_count == seq == 4 and local_len * seq == full_len

    def vec(v):
        return v.reshape(1, -1)

    def scalars(first):
        return jnp.stack([jnp.int32(first), jnp.int32(core), jnp.int32(me)])

    def exchange(parts):
        return [parts[0]] + [swap(parts[j], j, devices) for j in range(1, seq)]

    plain = scalars(0)
    def pick(values, j):
        return lax.dynamic_index_in_dim(values, me ^ j, 0, keepdims=False)

    distant = [pick(tokens, j) for j in (2, 3)]
    distant, [near] = together(distant, [tokens])
    chunks = exchange([pick(near, 0), pick(near, 1), *distant])
    norm1 = (vec(norm1_gain), vec(norm1_shift))
    weights = (w_query, w_key, w_value, vec(b_query), vec(b_value))

    ids = lax.dynamic_index_in_dim(segment_ids, me, 0, keepdims=False)
    digits = jnp.stack([(ids // BASE**n) % BASE for n in range(DIGITS)], 1)
    hot = (digits[:, :, None] == jnp.arange(BASE)[None, None, :]).reshape(full_len, CODE)
    hot = hot.astype(f32)
    rest = jnp.zeros((full_len, HALF - CODE), f32)
    query_code = jnp.concatenate([hot, rest], 1).astype(bf16).T
    key_code = jnp.concatenate([-1e30 * (1.0 - hot), rest.at[:, :3].set(1.0)], 1).astype(bf16)
    key_code = jnp.concatenate([key_code, key_code], 1)

    local_ids = lax.dynamic_slice_in_dim(segment_ids, me * local_len, local_len, 1)
    is_image = (local_ids != full_len).astype(bf16)[:, :, None]
    out_grad = grad_out * is_image
    grad_b_down = jnp.sum(out_grad.astype(f32), axis=(0, 1))

    before = qkv(scalars(pair), chunks[:2], *norm1, *weights, ())
    before = list(before)
    [before[0]], [out_grad] = together([before[0]], [out_grad])
    others = chunks[2:]
    down_in = exchange([pick(out_grad, j) for j in range(seq)])
    x, normedT, q, k, v = qkv(scalars(1 - pair), others, *norm1, *weights, before)
    oT, olo, aux = attend(q, k, v, query_code, key_code)
    nbits = devices.bit_length() - 1
    far = tuple(range(3, nbits))
    every = list(range(nbits - 1, -1, -1))
    block_out, (grad_b_up, rg, bg, gain2, shift2, bias_out), grad_down, grad_up0, grad_up1 = mlp(
        plain,
        devices,
        4,
        oT,
        x,
        w_out,
        vec(b_out),
        vec(norm2_gain),
        vec(norm2_shift),
        down_in,
        w_up,
        w_down,
        vec(b_up),
        vec(b_down),
    )
    biases, grads = [], []

    def backward(first, pairs, bg, before):
        got, bias, parts = attend_back(
            plain, devices, first, pairs, q, k, v, w_out, bg, oT, olo, aux, key_code, normedT, before
        )
        grads.append(got)
        biases.append(bias)
        return parts

    split = len(grad_down) == 2 and nbits == 5
    spots = every[:-1]

    def on_chip(pairs, carry):
        sends = [pair_[0] for pair_ in pairs]
        carry, sends = together(carry, sends)
        return carry, [swap(v, 1, devices) for v in sends]

    made = [grad_down, grad_up0, grad_up1]
    block_out = list(block_out)
    if split:
        [bg], came = on_chip(made, [bg])
    block_out[2:] = [swap(block_out[j], j, devices) for j in range(2, seq)]
    parts = backward(0, 2, bg, ())
    if split:
        (parts[0], bg, *block_out[2:]), came = together([parts[0], bg, *block_out[2:]], came)
        down, up0, up1 = ([keep, other] for (_, keep), other in zip(made, came))
        sum_a = Sum(devices, spots, [(down, 0, 3328)], [2, 1])
        sum_b = Sum(devices, spots, [(down, 3328, 768), (up1, 512, 2560)], [1, 2])
        sum_c = Sum(devices, spots, [(up0, 0, 2048), (up1, 0, 512)], [3, 4, 1, 2])
        sums = [sum_a, sum_b, sum_c]
        parts[0], bg = leave(sums, [parts[0], bg])
    block_out[1] = swap(block_out[1], 1, devices)
    parts = backward(2, 4, bg, parts)
    if split:
        parts[0], bg, *block_out = arrive(sums, [parts[0], bg, *block_out])
        parts[0], bg = leave(sums, [parts[0], bg])
    block_out = gather(plain, block_out)
    parts = backward(6, 2, bg, parts)
    gain = vec(norm1_gain)
    if split:
        parts[0], gain, block_out = arrive(sums, [parts[0], gain, block_out])
        [gain], came = on_chip([parts], [gain])
        sum_ab = sum_a.merged(sum_b, [3, 4])
        sums = [sum_ab, sum_c]
        [gain] = leave(sums, [gain])
        [gain], came = together([gain], came)
        ours = [parts[1], *came]
        cols = parts[1].shape[1] // 2
        sum_d = Sum(devices, spots, [(ours, 0, cols)], [2, 1])
        sum_e = Sum(devices, spots, [(ours, cols, cols)], [1, 2])
        [gain] = leave([sum_d, sum_e], [gain])
        sums += [sum_d, sum_e]
    *token, eight = token_grad(
        plain,
        grads,
        w_query,
        w_key,
        w_value,
        x,
        rg,
        gain,
        biases,
        [bias_out, gain2, shift2, vec(grad_b_down)],
    )
    own = width // devices
    eight = jnp.transpose(eight.reshape(8, devices, -1), (1, 0, 2)).reshape(devices, -1)
    vectors = jnp.concatenate([eight, grad_b_up.reshape(devices, -1)], 1)
    if split:
        token = arrive(sums, token)
        token = leave(sums, token)
        token[2] = swap(token[2], 2, devices)
        token = arrive([sum_ab, sum_c, sum_d, sum_e], token)
        both = sum_d.merged(sum_e, [])
        [blocks] = prepare([sum_ab, sum_c], [both.wanted(0, bf16, both.segments)])
        token, [blocks] = together(token, [blocks])
        along = [[d for d in range(devices) if d % 8 == low] for low in range(8)]
        blocks = lax.all_to_all(blocks, AXES, 0, 0, axis_index_groups=along, tiled=True)
    else:
        token[2] = swap(token[2], 2, devices)
    vectors = lax.all_to_all(vectors, AXES, 0, 0, tiled=True)
    token[1], token[3] = swap(token[1], 1, devices), swap(token[3], 3, devices)
    if split:
        width_in = blocks.shape[1]
        terms = [(blocks, [place // 2, place % 2], 0) for place in range(4)]
        grad_w_query, grad_w_key, grad_w_value = add_all(
            [(f32, both.chunk, 0, [(width_in, terms)], 3)]
        )
        down0, down1, up1 = sum_ab.total
        up0, up_mid = sum_c.total
        grad_w_down = jnp.concatenate([down0, down1], 1).reshape(own, -1, width)
        grad_w_down = jnp.transpose(grad_w_down, (1, 0, 2)).reshape(-1, width)
        at = up1.shape[1] - width
        grad_w_up = jnp.concatenate([up0, up_mid, up1[:, :at]], 1)
        grad_w_out = up1[:, at:]
    else:

        def over_all(values):
            return lax.psum_scatter(values.astype(f32), AXES, scatter_dimension=0, tiled=True)

        grad_w_down, up0, up1, qkv_sums = (over_all(pair_[0]) for pair_ in (*made, parts))
        qkv_sums = qkv_sums.reshape(own, width // 128, 3, 128)
        grad_w_query, grad_w_key, grad_w_value = (
            qkv_sums[:, :, n].reshape(own, width) for n in range(3)
        )
        grad_w_up = jnp.concatenate([up0, up1[:, : hidden - up0.shape[1]]], 1)
        grad_w_out = up1[:, hidden - up0.shape[1] :]
    vectors = jnp.sum(vectors, 0)
    grad_tokens = gather(plain, token)
    parts, start = [], 0
    for size in [width] * 8 + [hidden]:
        parts.append(vectors[start : start + size // devices])
        start += size // devices
    gain1, shift1, bq, bv, bo, gain2, shift2, bd, bu = parts
    return (
        block_out,
        grad_tokens,
        gain1,
        shift1,
        grad_w_query,
        bq,
        grad_w_key,
        grad_w_value,
        bv,
        grad_w_out,
        bo,
        gain2,
        shift2,
        grad_w_up,
        bu,
        grad_w_down,
        bd,
    )


def solution(mesh):
    tokens = P("rows", "seq", None)
    spread = P(("rows", "seq"))
    spread2 = P(("rows", "seq"), None)
    return jax.shard_map(
        on_device,
        mesh=mesh,
        in_specs=(tokens, P("rows", None), tokens) + (P(),) * 15,
        out_specs=(
            tokens,
            tokens,
            spread,
            spread,
            spread2,
            spread,
            spread2,
            spread2,
            spread,
            spread2,
            spread,
            spread,
            spread,
            spread2,
            spread,
            spread2,
            spread,
        ),
        check_vma=False,
    )
```

```python
import jax
import jax.numpy as jnp
import numpy as np
from jax import lax
from jax.experimental import pallas as pl
from jax.experimental.pallas import tpu as pltpu
from jax.sharding import PartitionSpec as P

HEADS = 16
norm_eps = 1e-06
bf16 = jnp.bfloat16
f32 = jnp.float32
MIB = 1024 * 1024
DIGITS, BASE = 3, 11
CODE = DIGITS * BASE
HALF = 64


def dg(a, b, ca, cb):
    return lax.dot_general(a, b, (((ca,), (cb,)), ((), ())), preferred_element_type=f32)


def params(mib):
    return pltpu.CompilerParams(vmem_limit_bytes=mib * MIB)


def cost(flops, bytes_accessed, transcendentals=0):
    return pl.CostEstimate(
        flops=20 * flops, bytes_accessed=20 * bytes_accessed, transcendentals=transcendentals
    )


def core_parts(grad, chunk, core):
    rows, cols = grad.shape
    runs = grad.reshape(rows // (2 * chunk), 2, chunk, cols)
    even = runs[:, 0].reshape(rows // 2, cols)
    odd = runs[:, 1].reshape(rows // 2, cols)
    first = core == 0
    return jnp.where(first, odd, even), jnp.where(first, even, odd)


def put_parts(refs, grad, chunk, core):
    if len(refs) == 1:
        refs[0][...] = grad.astype(bf16)
    else:
        other, own = core_parts(grad, chunk, core)
        refs[0][...] = other.astype(bf16)
        refs[1][...] = own.astype(bf16)


def full_spec(rows, cols):
    return pl.BlockSpec((rows, cols), lambda i, *_: (0, 0), pipeline_mode=pl.Buffered(1))


def call(kernel, scalars, grid, ins, in_specs, outs, out_specs, scratch=(), aliases=None, est=None, mib=60):
    return pl.pallas_call(
        kernel,
        grid_spec=pltpu.PrefetchScalarGridSpec(
            num_scalar_prefetch=1,
            grid=(grid,),
            in_specs=in_specs,
            out_specs=out_specs,
            scratch_shapes=list(scratch),
        ),
        out_shape=outs,
        input_output_aliases=aliases or {},
        compiler_params=params(mib),
        cost_estimate=est,
    )(scalars, *ins)


def norm_parts(values):
    mean = jnp.mean(values, axis=-1, keepdims=True)
    centered = values - mean
    variance = jnp.mean(centered * centered, axis=-1, keepdims=True)
    rstd = lax.rsqrt(variance + norm_eps)
    return centered * rstd, rstd


def qkv_kernel(s, c0, c1, gain, shift, wq, wk, wv, bq, bv, *refs):
    x, nT, q, k, v, n_scr = refs[-6:]
    length = c0.shape[0]
    core = s[1]

    @pl.when(pl.program_id(0) == 0)
    def _():
        for chunk, at in ((c0, core), (c1, 1 - core)):
            rows = pl.ds(pl.multiple_of(at * length, length), length)
            values = chunk[...]
            x[rows, :] = values
            n, _ = norm_parts(values.astype(f32))
            n_scr[rows, :] = (n * gain[...] + shift[...]).astype(bf16)

    n = n_scr[...]
    block = wq.shape[1]
    q[...] = (dg(n, wq[...], 1, 0) + bq[...]).astype(bf16) * 0.125
    k[...] = dg(n, wk[...], 1, 0).astype(bf16)
    v[...] = (dg(n, wv[...], 1, 0) + bv[...]).astype(bf16)
    nT[...] = n_scr[:, pl.ds(pl.multiple_of(pl.program_id(0) * block, block), block)].T


def qkv(scalars, chunks, gain, shift, wq, wk, wv, bq, bv, before):
    length, width = chunks[0].shape
    total = 4 * length
    block = 256
    whole = full_spec(length, width)
    vec = full_spec(1, width)
    part = pl.BlockSpec((width, block), lambda i, s: (0, i))
    bias = pl.BlockSpec((1, block), lambda i, s: (0, i))
    wide = pl.BlockSpec((2 * length, width), lambda i, s: (s[0], 0), pipeline_mode=pl.Buffered(1))
    rows = pl.BlockSpec((2 * length, block), lambda i, s: (s[0], i))
    cols = pl.BlockSpec((block, 2 * length), lambda i, s: (i, s[0]))
    out = pltpu.HBM((total, width), bf16)
    outT = pltpu.HBM((width, total), bf16)
    return call(
        qkv_kernel,
        scalars,
        width // block,
        [*chunks, gain, shift, wq, wk, wv, bq, bv, *before],
        [whole, whole, vec, vec, part, part, part, bias, bias]
        + [pl.BlockSpec(memory_space=pl.ANY)] * len(before),
        [out, outT, out, out, out],
        [wide, cols, rows, rows, rows],
        [pltpu.VMEM((2 * length, width), bf16)],
        aliases={10 + n: n for n in range(len(before))},
        mib=20,
        est=cost(2 * 2 * length * width * 3 * width, 20 * MIB),
    )


def pieces(value, row, base):
    hi = value.astype(bf16).astype(f32)
    mid = (value - hi).astype(bf16).astype(f32)
    low = value - hi - mid
    return jnp.where(
        row == CODE, hi, jnp.where(row == CODE + 1, mid, jnp.where(row == CODE + 2, low, base))
    )


def attend_kernel(q, k, v, fT, g, oT, olo, aux):
    total, wide = k.shape
    lane = lax.broadcasted_iota(jnp.int32, (total, 128), 1)
    row = lax.broadcasted_iota(jnp.int32, (HALF, total), 0)
    codes, queries_code = g[...], fT[...]
    ones = jnp.ones((16, total), bf16)
    qT, vT = q[...].T, v[...].T

    def score(h):
        keys = k[:, h // 2 * 128 : h // 2 * 128 + 128]
        ka = jnp.where((lane < HALF) == (h % 2 == 0), keys, codes)
        qh = qT[h * HALF : (h + 1) * HALF, :]
        qa = jnp.concatenate([qh, queries_code] if h % 2 == 0 else [queries_code, qh], 0)
        s = dg(ka, qa, 1, 0)
        return s, jnp.max(s, axis=0, keepdims=True)

    def finish(h, s, top):
        head = slice(h * HALF, (h + 1) * HALF)
        va = jnp.concatenate([vT[head, :], ones], 0)
        p = jnp.exp(s - top).astype(bf16)
        mixed = dg(va, p, 1, 0)
        weight = mixed[HALF : HALF + 1]
        out = mixed[:HALF] / weight
        low = out.astype(bf16)
        oT[head, :] = low
        olo[head, :] = (out - low.astype(f32)).astype(bf16)
        aux[head, :] = pieces(
            -(top + jnp.log(weight)), row, queries_code.astype(f32)
        ).astype(bf16)

    heads = wide // HALF
    ahead = score(0)
    for h in range(heads):
        here = ahead
        if h + 1 < heads:
            ahead = score(h + 1)
        finish(h, *here)


def attend(q, k, v, fT, g, wide=256):
    total, width = q.shape
    tall = pl.BlockSpec((total, wide), lambda i: (0, i))
    pair = pl.BlockSpec((wide, total), lambda i: (i, 0))
    return pl.pallas_call(
        attend_kernel,
        grid=(width // wide,),
        in_specs=[
            tall,
            tall,
            tall,
            pl.BlockSpec((HALF, total), lambda i: (0, 0)),
            pl.BlockSpec((total, 128), lambda i: (0, 0)),
        ],
        out_specs=[pair] * 3,
        out_shape=[jax.ShapeDtypeStruct((width, total), bf16)] * 3,
        compiler_params=params(60),
        cost_estimate=cost(16 * HEADS * total * total * 64, 12 * MIB, HEADS * total * total),
    )(q, k, v, fT, g)


def norm_back(n, rstd, grad, gain):
    gh = grad * gain
    mean = jnp.mean(gh, axis=-1, keepdims=True)
    tilt = jnp.mean(gh * n, axis=-1, keepdims=True)
    return rstd * (gh - mean - n * tilt)


def mlp_kernel(
    chunks, heads, cut, s, oT, x, wo, bo, gain, shift, wu, wd, bu, bd, *refs
):
    grads_in, outs = refs[:heads], refs[heads : 2 * heads]
    gbu, rg, bg, ggain, gshift, gb, *refs = refs[2 * heads :]
    step, steps = pl.program_id(0), pl.num_programs(0)
    per = (len(refs) - 6) // 3
    gwd, gwu0, gwu1 = refs[:per], refs[per : 2 * per], refs[2 * per : 3 * per]
    acc_o, acc_n, res, n2, di, oT_scr = refs[-6:]
    total = n2.shape[0]
    block = x.shape[0]
    after = steps - 2

    @pl.when(step < heads)
    def _():
        rows = pl.ds(pl.multiple_of(step * block, block), block)
        r = x[...].astype(f32) + dg(oT[...], wo[...], 0, 0) + bo[...]
        res[rows, :] = r
        acc_o[rows, :] = r + bd[...]
        n, _ = norm_parts(r)
        n2[rows, :] = (n * gain[...] + shift[...]).astype(bf16)
        oT_scr[:, rows] = oT[...]

    @pl.when(step == 0)
    def _():
        for j, ref in enumerate(grads_in):
            di[pl.ds(pl.multiple_of((s[2] ^ j) * block, block), block), :] = ref[...]

    @pl.when((step >= heads) & (step < after))
    def _():
        pre = dg(n2[...], wu[...], 1, 0) + bu[...]
        dact = dg(di[...], wd[...], 1, 1)
        cdf = 0.5 * (1.0 + lax.erf(pre * np.float32(np.sqrt(0.5))))
        pdf = jnp.exp(-0.5 * pre * pre) * np.float32(1 / np.sqrt(2 * np.pi))
        act = (pre * cdf).astype(bf16)
        acc_o[...] += dg(act, wd[...], 1, 0)
        hidden = (dact * (cdf + pre * pdf)).astype(bf16)
        new = dg(hidden, wu[...], 1, 1)

        @pl.when(step == heads)
        def _():
            acc_n[...] = new

        @pl.when(step > heads)
        def _():
            acc_n[...] += new

        down_grad = dg(act, di[...], 0, 0)
        if len(gwd) == 1:
            gwd[0][...] = down_grad.astype(bf16)
        else:
            rows, size = chunks
            width = down_grad.shape[1]
            for ref, part in zip(gwd, core_parts(down_grad, rows, s[1])):
                for at in range(0, part.shape[0], size):
                    device, place = at // rows, at % rows // size
                    ref[device * size : (device + 1) * size, place * width : (place + 1) * width] = (
                        part[at : at + size, :].astype(bf16)
                    )
        gbu[...] = jnp.sum(hidden.astype(f32), axis=0, keepdims=True)
        up_grad = dg(n2[...], hidden, 0, 0)

        @pl.when(step < heads + cut)
        def _():
            put_parts(gwu0, up_grad, chunks[1], s[1])

        @pl.when(step >= heads + cut)
        def _():
            put_parts(gwu1, up_grad, chunks[1], s[1])

    @pl.when(step == after)
    def _():
        for j, ref in enumerate(outs):
            rows = pl.ds(pl.multiple_of((s[2] ^ j) * block, block), block)
            ref[...] = acc_o[rows, :].astype(bf16)
        ggain[...] = jnp.zeros_like(ggain)
        gshift[...] = jnp.zeros_like(gshift)
        gb[...] = jnp.zeros_like(gb)

        @pl.loop(0, total // 256)
        def _(i):
            rows = pl.ds(pl.multiple_of(i * 256, 256), 256)
            n, rstd = norm_parts(res[rows, :])
            grad = acc_n[rows, :]
            ggain[...] += jnp.sum(grad * n, axis=0, keepdims=True)
            gshift[...] += jnp.sum(grad, axis=0, keepdims=True)
            resid = di[rows, :].astype(f32) + norm_back(n, rstd, grad, gain[...])
            rg[rows, :] = resid
            low = resid.astype(bf16)
            bg[rows, :] = low
            gb[...] += jnp.sum(low.astype(f32), axis=0, keepdims=True)

    @pl.when(step >= after)
    def _():
        half = bg.shape[1] // 2
        cols = pl.ds(pl.multiple_of((step - after) * half, half), half)
        put_parts(gwu1, dg(oT_scr[...], bg[:, cols], 1, 0), chunks[1], s[1])


def mlp(scalars, devices, cut, oT, x, wo, bo, gain, shift, di, wu, wd, bu, bd):
    total, width = x.shape
    hidden = wu.shape[1]
    rows_block, block = 256, 512
    heads = total // rows_block
    steps = hidden // block
    chunks = hidden // devices, width // devices
    parts = 2 if min(chunks) % 16 == 0 else 1
    down_shape = (width // 2, hidden) if parts == 2 else (hidden, width)
    full = full_spec(total, width)
    vec = full_spec(1, width)

    def early(i):
        return jnp.minimum(i, heads - 1)

    def late(i):
        return jnp.clip(i - heads, 0, steps - 1)

    tokens = pl.BlockSpec((rows_block, width), lambda i, s: (early(i), 0))
    up = pl.BlockSpec((width, block), lambda i, s: (0, late(i)))
    down = pl.BlockSpec((block, width), lambda i, s: (late(i), 0))
    bias = pl.BlockSpec((1, block), lambda i, s: (0, late(i)))
    row = jax.ShapeDtypeStruct((1, width), f32)
    got = call(
        lambda *refs: mlp_kernel(chunks, heads, cut, *refs),
        scalars,
        heads + steps + width // block,
        [oT, x, wo, bo, gain, shift, wu, wd, bu, bd, *di],
        [
            pl.BlockSpec((width, rows_block), lambda i, s: (0, early(i))),
            tokens,
            full_spec(width, width),
            vec,
            vec,
            vec,
            up,
            down,
            bias,
            vec,
        ]
        + [full_spec(rows_block, width)] * heads,
        [jax.ShapeDtypeStruct((rows_block, width), bf16)] * heads
        + [
            jax.ShapeDtypeStruct((1, hidden), f32),
            jax.ShapeDtypeStruct((total, width), f32),
            jax.ShapeDtypeStruct((total, width), bf16),
            row,
            row,
            row,
        ]
        + [jax.ShapeDtypeStruct(down_shape, bf16)] * parts
        + [jax.ShapeDtypeStruct((width // parts, cut * block), bf16)] * parts
        + [jax.ShapeDtypeStruct((width // parts, hidden - cut * block + width), bf16)] * parts,
        [full_spec(rows_block, width)] * heads
        + [bias, full, full, vec, vec, vec]
        + [pl.BlockSpec((down_shape[0] // steps, down_shape[1]), lambda i, s: (late(i), 0))] * parts
        + [
            pl.BlockSpec(
                (width // parts, block), lambda i, s: (0, jnp.clip(i - heads, 0, cut - 1))
            )
        ]
        * parts
        + [
            pl.BlockSpec(
                (width // parts, block), lambda i, s: (0, jnp.maximum(i - heads - cut, 0))
            )
        ]
        * parts,
        [
            pltpu.VMEM((total, width), f32),
            pltpu.VMEM((total, width), f32),
            pltpu.VMEM((total, width), f32),
            pltpu.VMEM((total, width), bf16),
            pltpu.VMEM((total, width), bf16),
            pltpu.VMEM((width, total), bf16),
        ],
        est=cost(2 * total * width * (6 * hidden + 2 * width), 70 * MIB, 2 * total * hidden),
    )
    outs, got = got[:heads], got[heads:]
    return outs, got[:6], got[6 : 6 + parts], got[6 + parts : 6 + 2 * parts], got[6 + 2 * parts :]


def attend_back_kernel(chunk, s, q, k, v, w, bg, oT, olo, aux, g, nT, *refs):
    dqT, dkT, dvT, bias, *grads = refs
    total = k.shape[0]
    lane = lax.broadcasted_iota(jnp.int32, (total, 128), 1)
    row = lax.broadcasted_iota(jnp.int32, (HALF, total), 0)
    keys, values, codes = k[...], v[...], g[...]
    qT, kT = q[...].T, keys.T
    doT = dg(w[...], bg[...], 1, 1).astype(bf16)
    parts = [[], [], []]
    for h in range(2):
        head = slice(h * HALF, (h + 1) * HALF)
        mine = (lane < HALF) == (h == 0)
        ka = jnp.where(mine, keys, codes)
        va = jnp.where(mine, values, codes)
        doh, qh, ax = doT[head, :], qT[head, :], aux[head, :]
        full = oT[head, :].astype(f32) + olo[head, :].astype(f32)
        delta = -jnp.sum(doh.astype(f32) * full, axis=0, keepdims=True)
        dx = pieces(delta, row, 0.0).astype(bf16)
        qa = jnp.concatenate([qh, ax] if h == 0 else [ax, qh], 0)
        doa = jnp.concatenate([doh, dx] if h == 0 else [dx, doh], 0)
        scores = dg(ka, qa, 1, 0)
        dp = dg(va, doa, 1, 0)
        p = jnp.exp(scores)
        low = p.astype(bf16)
        ds = (p * dp).astype(bf16)
        parts[1].append(dg(qh, ds, 1, 1).astype(bf16))
        parts[2].append(dg(doh, low, 1, 1).astype(bf16))
        parts[0].append((dg(kT[head, :], ds, 1, 0) * 0.125).astype(bf16))
    new = jnp.concatenate([p for pair in parts for p in pair], 0)
    for n, ref in enumerate((dqT, dkT, dvT)):
        ref[...] = new[128 * n : 128 * (n + 1)]
    put_parts(grads, dg(nT[...], new, 1, 1), chunk, s[1])
    bias[...] = dg(jnp.ones((8, total), bf16), new, 1, 1)[:1]


def attend_back(scalars, devices, first, pairs, q, k, v, w, bg, oT, olo, aux, g, nT, before):
    total, width = q.shape
    chunk = width // devices
    parts = 2 if chunk % 16 == 0 else 1
    pair = pl.BlockSpec((128, total), lambda i, s: (i + first, 0))
    tall = pl.BlockSpec((total, 128), lambda i, s: (0, i + first))
    done = pl.BlockSpec((128, total), lambda i, s: (i, 0))
    outs = call(
        lambda *refs: attend_back_kernel(chunk, *refs[:11], *refs[11 + len(before) :]),
        scalars,
        pairs,
        [q, k, v, w, bg, oT, olo, aux, g, nT, *before],
        [tall, tall, tall, pl.BlockSpec((128, width), lambda i, s: (i + first, 0))]
        + [full_spec(total, width), pair, pair, pair]
        + [full_spec(total, 128), full_spec(width, total)]
        + [pl.BlockSpec(memory_space=pl.ANY)] * len(before),
        [jax.ShapeDtypeStruct((128 * pairs, total), bf16)] * 3
        + [jax.ShapeDtypeStruct((1, 384 * pairs), f32)]
        + [jax.ShapeDtypeStruct((width // parts, 3 * width), bf16)] * parts,
        [done] * 3
        + [pl.BlockSpec((1, 384), lambda i, s: (0, i))]
        + [pl.BlockSpec((width // parts, 384), lambda i, s: (0, i + first))] * parts,
        aliases={11 + n: 4 + n for n in range(len(before))},
        est=cost(pairs * 100 * 2 * total * total * 64, pairs * 3 * MIB, pairs * 2 * total * total),
    )
    return outs[:3], outs[3], list(outs[4:])


def token_grad_kernel(count, groups, s, *refs):
    grads = refs[:count]
    wq, wk, wv, x, rg, gain, *more = refs[count:-6]
    outs, eight, acc = refs[-6:-2], refs[-2], refs[-1]
    biases, rows = more[:groups], more[groups:]
    step = pl.program_id(0)

    @pl.when(step == 0)
    def _():
        eight[...] = jnp.zeros_like(eight)
        acc[...] = jnp.zeros_like(acc)
        for n, ref in enumerate(rows):
            eight[4 + n : 5 + n, :] = ref[...]
        at = 0
        for ref in biases:
            for n in range(ref.shape[1] // 384):
                eight[2:3, at : at + 128] = ref[:, 384 * n : 384 * n + 128]
                eight[3:4, at : at + 128] = ref[:, 384 * n + 256 : 384 * n + 384]
                at += 128

    grad = acc[...]
    new = 0.0
    for n, w in enumerate((wq, wk, wv)):
        new = new + dg(jnp.concatenate([g[...] for g in grads[n::3]], 0), w[...], 0, 1)
    n, rstd = norm_parts(x[...].astype(f32))
    eight[0:1, :] += jnp.sum(grad * n, axis=0, keepdims=True)
    eight[1:2, :] += jnp.sum(grad, axis=0, keepdims=True)
    done = (rg[...] + norm_back(n, rstd, grad, gain[...])).astype(bf16)
    for j, out in enumerate(outs):

        @pl.when((step - 1) == (s[2] ^ j))
        def _(out=out):
            out[...] = done

    acc[...] = new


def token_grad(scalars, grads, wq, wk, wv, x, rg, gain, biases, rows):
    total, width = x.shape
    block = 256
    steps = total // block
    grads = [g for triple in grads for g in triple]

    def now(i):
        return jnp.minimum(i, steps - 1)

    def past(i):
        return jnp.maximum(i - 1, 0)

    tokens = pl.BlockSpec((block, width), lambda i, s: (past(i), 0))
    vec = full_spec(1, width)
    return call(
        lambda *refs: token_grad_kernel(len(grads), len(biases), *refs),
        scalars,
        steps + 1,
        [*grads, wq, wk, wv, x, rg, gain, *biases, *rows],
        [pl.BlockSpec((g.shape[0], block), lambda i, s: (0, now(i))) for g in grads]
        + [full_spec(width, width)] * 3
        + [tokens, tokens, vec]
        + [full_spec(*b.shape) for b in biases]
        + [vec] * len(rows),
        [jax.ShapeDtypeStruct((block, width), bf16)] * steps
        + [jax.ShapeDtypeStruct((8, width), f32)],
        [full_spec(block, width)] * steps + [full_spec(8, width)],
        [pltpu.VMEM((block, width), f32)],
        est=cost(6 * total * width * width, 24 * MIB),
    )


def gather_kernel(s, *refs):
    parts, (out, sems) = refs[:-2], refs[-2:]
    copies = [
        pltpu.make_async_copy(ref, out.at[s[2] ^ j], sems.at[j]) for j, ref in enumerate(parts)
    ]
    for copy in copies:
        copy.start()
    for copy in copies:
        copy.wait()


def gather(scalars, parts):
    return call(
        gather_kernel,
        scalars,
        1,
        parts,
        [full_spec(*part.shape) for part in parts],
        jax.ShapeDtypeStruct((len(parts), *parts[0].shape), parts[0].dtype),
        pl.BlockSpec(memory_space=pl.ANY),
        [pltpu.SemaphoreType.DMA((len(parts),))],
    )


AXES = ("rows", "seq")


def swap(values, mask, devices):
    return lax.ppermute(values, AXES, [(d, d ^ mask) for d in range(devices)])


def add_kernel(jobs, arrays, s, *refs):
    many = sum(count_out for _, _, count_out in jobs)
    ins, outs = refs[:arrays], refs[arrays : arrays + many]
    refs = list(refs[arrays + many :])
    sem_in, sem_out = refs[-2:]
    loads, stores, at, count, first_out = [], [], 0, 0, 0
    for job, (free, segments, count_out) in enumerate(jobs):
        result = refs[at : at + count_out]
        at += count_out
        places = []
        for width, terms in segments:
            places.append((width, refs[at : at + len(terms)]))
            at += len(terms)
        for piece in range(2 if free else 1):
            copies = []
            for (width, terms), (_, buffers) in zip(segments, places):
                for buffer, (array, index, column) in zip(buffers, terms):
                    where, first = [], True
                    for entry in index:
                        if entry is None:
                            where.append(piece if first else slice(None))
                            first = False
                        else:
                            where.append(s[entry])
                    where += [slice(None), pl.ds(column, width)]
                    copies.append(
                        pltpu.make_async_copy(
                            ins[array].at[tuple(where)],
                            buffer.at[piece] if free else buffer,
                            sem_in.at[count],
                        )
                    )
                    copies[-1].start()
                    count += 1
            loads.append((outs[first_out : first_out + count_out], piece, free, places, result, copies))
        first_out += count_out
    for targets, piece, free, places, result, copies in loads:
        for copy in copies:
            copy.wait()
        for n in range(2 ** max(free - 1, 0)):
            here = ((piece,) if free else ()) + tuple(n >> b & 1 for b in range(free - 1))
            column = 0
            for width, buffers in places:
                total = sum(buffer[here].astype(f32) for buffer in buffers)
                total = total.astype(result[0].dtype)
                if len(result) == 1:
                    result[0][here + (slice(None), slice(column, column + width))] = total
                else:
                    for block in range(0, width, 128):
                        turn, which = divmod((column + block) // 128, len(result))
                        result[which][:, 128 * turn : 128 * (turn + 1)] = total[:, block : block + 128]
                column += width
        for buffer, target in zip(result, targets):
            stores.append(
                pltpu.make_async_copy(
                    buffer.at[piece] if free else buffer,
                    target.at[piece] if free else target,
                    sem_out.at[len(stores)],
                )
            )
            stores[-1].start()
    for copy in stores:
        copy.wait()


def add_all(table, wanted):
    arrays, jobs, scratch, outs, shapes = [], [], [], [], []
    copies = pieces_out = 0
    for dtype, chunk, free, segments, count_out in wanted:
        shape = (2,) * free + (chunk, sum(width for width, _ in segments) // count_out)
        scratch += [pltpu.VMEM(shape, dtype)] * count_out
        outs += [jax.ShapeDtypeStruct(shape, dtype)] * count_out
        pieces_out += 2 if free else count_out
        listed = []
        for width, terms in segments:
            row = []
            for array, index, column in terms:
                found = [n for n, other in enumerate(arrays) if other is array]
                if not found:
                    arrays.append(array)
                    shapes.append((2,) * len(index) + (chunk, array.shape[-1]))
                row.append((found[0] if found else len(arrays) - 1, index, column))
                scratch.append(pltpu.VMEM((2,) * free + (chunk, width), array.dtype))
                copies += 2 if free else 1
            listed.append((width, row))
        jobs.append((free, listed, count_out))
    anyspec = pl.BlockSpec(memory_space=pl.ANY)
    got = call(
        lambda *refs: add_kernel(jobs, len(arrays), *refs),
        table,
        1,
        [array.reshape(shape) for array, shape in zip(arrays, shapes)],
        [anyspec] * len(arrays),
        outs,
        [anyspec] * len(outs),
        scratch + [pltpu.SemaphoreType.DMA((copies,)), pltpu.SemaphoreType.DMA((pieces_out,))],
    )
    return [values.reshape(-1, values.shape[-1]) for values in got]


class Sum:
    def __init__(self, net, spots, segments, order):
        self.net, self.spots, self.order = net, list(spots), list(order)
        self.devices, self.table = net
        self.sending, self.coming, self.taken, self.total, self.shares = [], [], [], None, 1
        if segments:
            self.chunk = segments[0][0][0].shape[0] >> len(self.spots)
        self.segments = [
            (width, [(array, list(self.spots), column) for array in arrays])
            for arrays, column, width in segments
        ]

    def merged(self, other, order):
        new = Sum(self.net, self.spots, [], order)
        new.chunk, new.taken = self.chunk, list(self.taken)
        new.segments = self.segments + other.segments
        return new

    def wanted(self, mask, dtype, segments):
        nbits = self.devices.bit_length() - 1
        bits = {bit: bit + nbits * (mask >> bit & 1) for bit in self.taken}
        listed = [
            (width, [(v, [bits.get(bit) for bit in spots], column) for v, spots, column in terms])
            for width, terms in segments
        ]
        return (dtype, self.chunk, len(self.spots), listed, self.shares if dtype == f32 else 1)

    def masks(self):
        step = self.order.pop(0)
        bits = step if isinstance(step, tuple) else (step,)
        masks = [0]
        for bit in bits:
            masks += [m | 1 << bit for m in masks]
        self.taken += bits
        for bit in bits:
            self.spots.remove(bit)
        return masks[1:]

    def start(self):
        self.coming += [swap(v, mask, self.devices) for mask, v in self.sending]
        self.sending = []

    def arrive(self, coming):
        column = 0
        for width, terms in self.segments:
            terms += [(v, list(self.spots), column) for v in coming]
            column += width
        self.coming = []


def prepare(sums, more=()):
    jobs = []
    for t in sums:
        if t.order:
            jobs += [(t, mask, bf16, t.segments) for mask in t.masks()]
        elif t.total is None:
            whole = [t.segments] if t.shares > 1 else [[segment] for segment in t.segments]
            jobs += [(t, 0, f32, segments) for segments in whole]
            t.total = []
    if not jobs and not more:
        return []
    got = add_all(sums[0].table, [t.wanted(mask, dtype, segments) for t, mask, dtype, segments in jobs] + list(more))
    for t, mask, dtype, _ in jobs:
        if dtype == f32:
            t.total += got[: t.shares]
            got = got[t.shares :]
        else:
            t.sending.append((mask, got[0]))
            got = got[1:]
    return got


def together(*groups):
    flat = lax.optimization_barrier(tuple(v for group in groups for v in group))
    out, start = [], 0
    for group in groups:
        out.append(list(flat[start : start + len(group)]))
        start += len(group)
    return out


def arrive(sums, carry):
    got = together(carry, *[t.coming for t in sums])
    for t, coming in zip(sums, got[1:]):
        t.arrive(coming)
    return got[0]


def leave(sums, carry):
    prepare(sums)
    got = together(carry, *[[v for _, v in t.sending] for t in sums])
    for t, sending in zip(sums, got[1:]):
        t.sending = [(mask, v) for (mask, _), v in zip(t.sending, sending)]
        t.start()
    return got[0]


def on_device(
    tokens,
    segment_ids,
    grad_out,
    norm1_gain,
    norm1_shift,
    w_query,
    b_query,
    w_key,
    w_value,
    b_value,
    w_out,
    b_out,
    norm2_gain,
    norm2_shift,
    w_up,
    b_up,
    w_down,
    b_down,
):
    row_count, local_len, width = tokens.shape
    full_len = segment_ids.shape[1]
    hidden = w_up.shape[1]
    seq, rows = lax.axis_size("seq"), lax.axis_size("rows")
    devices = rows * seq
    me = lax.axis_index("seq")
    core, pair = me % 2, me // 2
    assert row_count == seq == 4 and local_len * seq == full_len

    def vec(v):
        return v.reshape(1, -1)

    def scalars(first):
        return jnp.stack([jnp.int32(first), jnp.int32(core), jnp.int32(me)])

    def exchange(parts):
        return [parts[0]] + [swap(parts[j], j, devices) for j in range(1, seq)]

    plain = scalars(0)
    def pick(values, j):
        return lax.dynamic_index_in_dim(values, me ^ j, 0, keepdims=False)

    distant = [pick(tokens, j) for j in (2, 3)]
    distant, [near] = together(distant, [tokens])
    chunks = exchange([pick(near, 0), pick(near, 1), *distant])
    norm1 = (vec(norm1_gain), vec(norm1_shift))
    weights = (w_query, w_key, w_value, vec(b_query), vec(b_value))

    ids = lax.dynamic_index_in_dim(segment_ids, me, 0, keepdims=False)
    digits = jnp.stack([(ids // BASE**n) % BASE for n in range(DIGITS)], 1)
    hot = (digits[:, :, None] == jnp.arange(BASE)[None, None, :]).reshape(full_len, CODE)
    hot = hot.astype(f32)
    rest = jnp.zeros((full_len, HALF - CODE), f32)
    query_code = jnp.concatenate([hot, rest], 1).astype(bf16).T
    key_code = jnp.concatenate([-1e30 * (1.0 - hot), rest.at[:, :3].set(1.0)], 1).astype(bf16)
    key_code = jnp.concatenate([key_code, key_code], 1)

    local_ids = lax.dynamic_slice_in_dim(segment_ids, me * local_len, local_len, 1)
    is_image = (local_ids != full_len).astype(bf16)[:, :, None]
    out_grad = grad_out * is_image
    grad_b_down = jnp.sum(out_grad.astype(f32), axis=(0, 1))

    before = qkv(scalars(pair), chunks[:2], *norm1, *weights, ())
    before = list(before)
    [before[0]], [out_grad] = together([before[0]], [out_grad])
    others = chunks[2:]
    down_in = exchange([pick(out_grad, j) for j in range(seq)])
    x, normedT, q, k, v = qkv(scalars(1 - pair), others, *norm1, *weights, before)
    oT, olo, aux = attend(q, k, v, query_code, key_code)
    nbits = devices.bit_length() - 1
    far = tuple(range(3, nbits))
    every = list(range(nbits - 1, -1, -1))
    block_out, (grad_b_up, rg, bg, gain2, shift2, bias_out), grad_down, grad_up0, grad_up1 = mlp(
        plain,
        devices,
        4,
        oT,
        x,
        w_out,
        vec(b_out),
        vec(norm2_gain),
        vec(norm2_shift),
        down_in,
        w_up,
        w_down,
        vec(b_up),
        vec(b_down),
    )
    biases, grads = [], []

    def backward(first, pairs, bg, before):
        got, bias, parts = attend_back(
            plain, devices, first, pairs, q, k, v, w_out, bg, oT, olo, aux, key_code, normedT, before
        )
        grads.append(got)
        biases.append(bias)
        return parts

    split = len(grad_down) == 2 and nbits == 5
    own_bits = [lax.axis_index(AXES) >> n & 1 for n in range(nbits)]
    table = jnp.stack([jnp.int32(n) for n in (*own_bits, *(1 - n for n in own_bits), 0, 1)])
    net = devices, table
    spots = every[:-1]

    def on_chip(pairs, carry):
        sends = [pair_[0] for pair_ in pairs]
        carry, sends = together(carry, sends)
        return carry, [swap(v, 1, devices) for v in sends]

    made = [grad_down, grad_up0, grad_up1]
    block_out = list(block_out)
    if split:
        [bg], came = on_chip(made, [bg])
    block_out[2:] = [swap(block_out[j], j, devices) for j in range(2, seq)]
    parts = backward(0, 2, bg, ())
    if split:
        (parts[0], bg, *block_out[2:]), came = together([parts[0], bg, *block_out[2:]], came)
        down, up0, up1 = ([keep, other] for (_, keep), other in zip(made, came))
        sum_a = Sum(net, spots, [(down, 0, 3328)], [2, 1])
        sum_b = Sum(net, spots, [(down, 3328, 768), (up1, 512, 2560)], [1, 2])
        sum_c = Sum(net, spots, [(up0, 0, 2048), (up1, 0, 512)], [3, 4, 1, 2])
        sums = [sum_a, sum_b, sum_c]
        parts[0], bg = leave(sums, [parts[0], bg])
    block_out[1] = swap(block_out[1], 1, devices)
    parts = backward(2, 4, bg, parts)
    if split:
        parts[0], bg, *block_out = arrive(sums, [parts[0], bg, *block_out])
        parts[0], bg = leave(sums, [parts[0], bg])
    block_out = gather(plain, block_out)
    parts = backward(6, 2, bg, parts)
    gain = vec(norm1_gain)
    if split:
        parts[0], gain, block_out = arrive(sums, [parts[0], gain, block_out])
        [gain], came = on_chip([parts], [gain])
        sum_ab = sum_a.merged(sum_b, [3, 4])
        sums = [sum_ab, sum_c]
        [gain] = leave(sums, [gain])
        [gain], came = together([gain], came)
        ours = [parts[1], *came]
        cols = parts[1].shape[1] // 2
        sum_d = Sum(net, spots, [(ours, 0, cols)], [2, 1])
        sum_e = Sum(net, spots, [(ours, cols, cols)], [1, 2])
        [gain] = leave([sum_d, sum_e], [gain])
        sums += [sum_d, sum_e]
    *token, eight = token_grad(
        plain,
        grads,
        w_query,
        w_key,
        w_value,
        x,
        rg,
        gain,
        biases,
        [bias_out, gain2, shift2, vec(grad_b_down)],
    )
    own = width // devices
    eight = jnp.transpose(eight.reshape(8, devices, -1), (1, 0, 2)).reshape(devices, -1)
    vectors = jnp.concatenate([eight, grad_b_up.reshape(devices, -1)], 1)
    if split:
        token = arrive(sums, token)
        token = leave(sums, token)
        token[2] = swap(token[2], 2, devices)
        token = arrive([sum_ab, sum_c, sum_d, sum_e], token)
        both = sum_d.merged(sum_e, [])
        [blocks] = prepare([sum_ab, sum_c], [both.wanted(0, bf16, both.segments)])
        token, [blocks] = together(token, [blocks])
        along = [[d for d in range(devices) if d % 8 == low] for low in range(8)]
        blocks = lax.all_to_all(blocks, AXES, 0, 0, axis_index_groups=along, tiled=True)
    else:
        token[2] = swap(token[2], 2, devices)
    vectors = lax.all_to_all(vectors, AXES, 0, 0, tiled=True)
    token[1], token[3] = swap(token[1], 1, devices), swap(token[3], 3, devices)
    if split:
        width_in = blocks.shape[1]
        zero = 2 * nbits
        terms = [(blocks, [zero + place // 2, zero + place % 2], 0) for place in range(4)]
        grad_w_query, grad_w_key, grad_w_value = add_all(
            table, [(f32, both.chunk, 0, [(width_in, terms)], 3)]
        )
        down0, down1, up1 = sum_ab.total
        up0, up_mid = sum_c.total
        grad_w_down = jnp.concatenate([down0, down1], 1).reshape(own, -1, width)
        grad_w_down = jnp.transpose(grad_w_down, (1, 0, 2)).reshape(-1, width)
        at = up1.shape[1] - width
        grad_w_up = jnp.concatenate([up0, up_mid, up1[:, :at]], 1)
        grad_w_out = up1[:, at:]
    else:

        def over_all(values):
            return lax.psum_scatter(values.astype(f32), AXES, scatter_dimension=0, tiled=True)

        grad_w_down, up0, up1, qkv_sums = (over_all(pair_[0]) for pair_ in (*made, parts))
        qkv_sums = qkv_sums.reshape(own, width // 128, 3, 128)
        grad_w_query, grad_w_key, grad_w_value = (
            qkv_sums[:, :, n].reshape(own, width) for n in range(3)
        )
        grad_w_up = jnp.concatenate([up0, up1[:, : hidden - up0.shape[1]]], 1)
        grad_w_out = up1[:, hidden - up0.shape[1] :]
    vectors = jnp.sum(vectors, 0)
    grad_tokens = gather(plain, token)
    parts, start = [], 0
    for size in [width] * 8 + [hidden]:
        parts.append(vectors[start : start + size // devices])
        start += size // devices
    gain1, shift1, bq, bv, bo, gain2, shift2, bd, bu = parts
    return (
        block_out,
        grad_tokens,
        gain1,
        shift1,
        grad_w_query,
        bq,
        grad_w_key,
        grad_w_value,
        bv,
        grad_w_out,
        bo,
        gain2,
        shift2,
        grad_w_up,
        bu,
        grad_w_down,
        bd,
    )


def solution(mesh):
    tokens = P("rows", "seq", None)
    spread = P(("rows", "seq"))
    spread2 = P(("rows", "seq"), None)
    return jax.shard_map(
        on_device,
        mesh=mesh,
        in_specs=(tokens, P("rows", None), tokens) + (P(),) * 15,
        out_specs=(
            tokens,
            tokens,
            spread,
            spread,
            spread2,
            spread,
            spread2,
            spread2,
            spread,
            spread2,
            spread,
            spread,
            spread,
            spread2,
            spread,
            spread2,
            spread,
        ),
        check_vma=False,
    )
```

```python
import jax
import jax.numpy as jnp
import numpy as np
from jax import lax
from jax.experimental import pallas as pl
from jax.experimental.pallas import tpu as pltpu
from jax.sharding import PartitionSpec as P

HEADS = 16
norm_eps = 1e-06
bf16 = jnp.bfloat16
f32 = jnp.float32
MIB = 1024 * 1024
DIGITS, BASE = 3, 11
CODE = DIGITS * BASE
HALF = 64


def dg(a, b, ca, cb):
    return lax.dot_general(a, b, (((ca,), (cb,)), ((), ())), preferred_element_type=f32)


def params(mib):
    return pltpu.CompilerParams(vmem_limit_bytes=mib * MIB)


def cost(flops, bytes_accessed, transcendentals=0):
    return pl.CostEstimate(
        flops=20 * flops, bytes_accessed=20 * bytes_accessed, transcendentals=transcendentals
    )


def core_parts(grad, chunk, core):
    rows, cols = grad.shape
    runs = grad.reshape(rows // (2 * chunk), 2, chunk, cols)
    even = runs[:, 0].reshape(rows // 2, cols)
    odd = runs[:, 1].reshape(rows // 2, cols)
    first = core == 0
    return jnp.where(first, odd, even), jnp.where(first, even, odd)


def put_parts(refs, grad, chunk, core):
    if len(refs) == 1:
        refs[0][...] = grad.astype(bf16)
    else:
        other, own = core_parts(grad, chunk, core)
        refs[0][...] = other.astype(bf16)
        refs[1][...] = own.astype(bf16)


def full_spec(rows, cols):
    return pl.BlockSpec((rows, cols), lambda i, *_: (0, 0), pipeline_mode=pl.Buffered(1))


def call(kernel, scalars, grid, ins, in_specs, outs, out_specs, scratch=(), aliases=None, est=None, mib=60):
    return pl.pallas_call(
        kernel,
        grid_spec=pltpu.PrefetchScalarGridSpec(
            num_scalar_prefetch=1,
            grid=(grid,),
            in_specs=in_specs,
            out_specs=out_specs,
            scratch_shapes=list(scratch),
        ),
        out_shape=outs,
        input_output_aliases=aliases or {},
        compiler_params=params(mib),
        cost_estimate=est,
    )(scalars, *ins)


def norm_parts(values):
    mean = jnp.mean(values, axis=-1, keepdims=True)
    centered = values - mean
    variance = jnp.mean(centered * centered, axis=-1, keepdims=True)
    rstd = lax.rsqrt(variance + norm_eps)
    return centered * rstd, rstd


def qkv_kernel(s, c0, c1, gain, shift, wq, wk, wv, bq, bv, *refs):
    x, nT, q, k, v, n_scr = refs[-6:]
    length = c0.shape[0]
    core = s[1]

    @pl.when(pl.program_id(0) == 0)
    def _():
        for chunk, at in ((c0, core), (c1, 1 - core)):
            rows = pl.ds(pl.multiple_of(at * length, length), length)
            values = chunk[...]
            x[rows, :] = values
            n, _ = norm_parts(values.astype(f32))
            n_scr[rows, :] = (n * gain[...] + shift[...]).astype(bf16)

    n = n_scr[...]
    block = wq.shape[1]
    q[...] = (dg(n, wq[...], 1, 0) + bq[...]).astype(bf16) * 0.125
    k[...] = dg(n, wk[...], 1, 0).astype(bf16)
    v[...] = (dg(n, wv[...], 1, 0) + bv[...]).astype(bf16)
    nT[...] = n_scr[:, pl.ds(pl.multiple_of(pl.program_id(0) * block, block), block)].T


def qkv(scalars, chunks, gain, shift, wq, wk, wv, bq, bv, before):
    length, width = chunks[0].shape
    total = 4 * length
    block = 256
    whole = full_spec(length, width)
    vec = full_spec(1, width)
    part = pl.BlockSpec((width, block), lambda i, s: (0, i))
    bias = pl.BlockSpec((1, block), lambda i, s: (0, i))
    wide = pl.BlockSpec((2 * length, width), lambda i, s: (s[0], 0), pipeline_mode=pl.Buffered(1))
    rows = pl.BlockSpec((2 * length, block), lambda i, s: (s[0], i))
    cols = pl.BlockSpec((block, 2 * length), lambda i, s: (i, s[0]))
    out = pltpu.HBM((total, width), bf16)
    outT = pltpu.HBM((width, total), bf16)
    return call(
        qkv_kernel,
        scalars,
        width // block,
        [*chunks, gain, shift, wq, wk, wv, bq, bv, *before],
        [whole, whole, vec, vec, part, part, part, bias, bias]
        + [pl.BlockSpec(memory_space=pl.ANY)] * len(before),
        [out, outT, out, out, out],
        [wide, cols, rows, rows, rows],
        [pltpu.VMEM((2 * length, width), bf16)],
        aliases={10 + n: n for n in range(len(before))},
        mib=20,
        est=cost(2 * 2 * length * width * 3 * width, 20 * MIB),
    )


def pieces(value, row, base):
    hi = value.astype(bf16).astype(f32)
    mid = (value - hi).astype(bf16).astype(f32)
    low = value - hi - mid
    return jnp.where(
        row == CODE, hi, jnp.where(row == CODE + 1, mid, jnp.where(row == CODE + 2, low, base))
    )


def attend_kernel(q, k, v, fT, g, oT, olo, aux):
    total, wide = k.shape
    lane = lax.broadcasted_iota(jnp.int32, (total, 128), 1)
    row = lax.broadcasted_iota(jnp.int32, (HALF, total), 0)
    codes, queries_code = g[...], fT[...]
    ones = jnp.ones((16, total), bf16)
    qT, vT = q[...].T, v[...].T

    def score(h):
        keys = k[:, h // 2 * 128 : h // 2 * 128 + 128]
        ka = jnp.where((lane < HALF) == (h % 2 == 0), keys, codes)
        qh = qT[h * HALF : (h + 1) * HALF, :]
        qa = jnp.concatenate([qh, queries_code] if h % 2 == 0 else [queries_code, qh], 0)
        s = dg(ka, qa, 1, 0)
        return s, jnp.max(s, axis=0, keepdims=True)

    def finish(h, s, top):
        head = slice(h * HALF, (h + 1) * HALF)
        va = jnp.concatenate([vT[head, :], ones], 0)
        p = jnp.exp(s - top).astype(bf16)
        mixed = dg(va, p, 1, 0)
        weight = mixed[HALF : HALF + 1]
        out = mixed[:HALF] / weight
        low = out.astype(bf16)
        oT[head, :] = low
        olo[head, :] = (out - low.astype(f32)).astype(bf16)
        aux[head, :] = pieces(
            -(top + jnp.log(weight)), row, queries_code.astype(f32)
        ).astype(bf16)

    heads = wide // HALF
    ahead = score(0)
    for h in range(heads):
        here = ahead
        if h + 1 < heads:
            ahead = score(h + 1)
        finish(h, *here)


def attend(q, k, v, fT, g, wide=256):
    total, width = q.shape
    tall = pl.BlockSpec((total, wide), lambda i: (0, i))
    pair = pl.BlockSpec((wide, total), lambda i: (i, 0))
    return pl.pallas_call(
        attend_kernel,
        grid=(width // wide,),
        in_specs=[
            tall,
            tall,
            tall,
            pl.BlockSpec((HALF, total), lambda i: (0, 0)),
            pl.BlockSpec((total, 128), lambda i: (0, 0)),
        ],
        out_specs=[pair] * 3,
        out_shape=[jax.ShapeDtypeStruct((width, total), bf16)] * 3,
        compiler_params=params(60),
        cost_estimate=cost(16 * HEADS * total * total * 64, 12 * MIB, HEADS * total * total),
    )(q, k, v, fT, g)


def norm_back(n, rstd, grad, gain):
    gh = grad * gain
    mean = jnp.mean(gh, axis=-1, keepdims=True)
    tilt = jnp.mean(gh * n, axis=-1, keepdims=True)
    return rstd * (gh - mean - n * tilt)


def mlp_kernel(
    chunks, heads, cut, s, oT, x, wo, bo, gain, shift, wu, wd, bu, bd, *refs
):
    grads_in, outs = refs[:heads], refs[heads : 2 * heads]
    gbu, rg, bg, ggain, gshift, gb, *refs = refs[2 * heads :]
    step, steps = pl.program_id(0), pl.num_programs(0)
    per = (len(refs) - 6) // 3
    gwd, gwu0, gwu1 = refs[:per], refs[per : 2 * per], refs[2 * per : 3 * per]
    acc_o, acc_n, res, n2, di, oT_scr = refs[-6:]
    total = n2.shape[0]
    block = x.shape[0]
    after = steps - 2

    @pl.when(step < heads)
    def _():
        rows = pl.ds(pl.multiple_of(step * block, block), block)
        r = x[...].astype(f32) + dg(oT[...], wo[...], 0, 0) + bo[...]
        res[rows, :] = r
        acc_o[rows, :] = r + bd[...]
        n, _ = norm_parts(r)
        n2[rows, :] = (n * gain[...] + shift[...]).astype(bf16)
        oT_scr[:, rows] = oT[...]

    @pl.when(step == 0)
    def _():
        for j, ref in enumerate(grads_in):
            di[pl.ds(pl.multiple_of((s[2] ^ j) * block, block), block), :] = ref[...]

    @pl.when((step >= heads) & (step < after))
    def _():
        pre = dg(n2[...], wu[...], 1, 0) + bu[...]
        dact = dg(di[...], wd[...], 1, 1)
        cdf = 0.5 * (1.0 + lax.erf(pre * np.float32(np.sqrt(0.5))))
        pdf = jnp.exp(-0.5 * pre * pre) * np.float32(1 / np.sqrt(2 * np.pi))
        act = (pre * cdf).astype(bf16)
        acc_o[...] += dg(act, wd[...], 1, 0)
        hidden = (dact * (cdf + pre * pdf)).astype(bf16)
        new = dg(hidden, wu[...], 1, 1)

        @pl.when(step == heads)
        def _():
            acc_n[...] = new

        @pl.when(step > heads)
        def _():
            acc_n[...] += new

        down_grad = dg(act, di[...], 0, 0)
        if len(gwd) == 1:
            gwd[0][...] = down_grad.astype(bf16)
        else:
            rows, size = chunks
            width = down_grad.shape[1]
            for ref, part in zip(gwd, core_parts(down_grad, rows, s[1])):
                for at in range(0, part.shape[0], size):
                    device, place = at // rows, at % rows // size
                    ref[device * size : (device + 1) * size, place * width : (place + 1) * width] = (
                        part[at : at + size, :].astype(bf16)
                    )
        gbu[...] = jnp.sum(hidden.astype(f32), axis=0, keepdims=True)
        up_grad = dg(n2[...], hidden, 0, 0)

        @pl.when(step < heads + cut)
        def _():
            put_parts(gwu0, up_grad, chunks[1], s[1])

        @pl.when(step >= heads + cut)
        def _():
            put_parts(gwu1, up_grad, chunks[1], s[1])

    @pl.when(step == after)
    def _():
        for j, ref in enumerate(outs):
            rows = pl.ds(pl.multiple_of((s[2] ^ j) * block, block), block)
            ref[...] = acc_o[rows, :].astype(bf16)
        ggain[...] = jnp.zeros_like(ggain)
        gshift[...] = jnp.zeros_like(gshift)
        gb[...] = jnp.zeros_like(gb)

        @pl.loop(0, total // 256)
        def _(i):
            rows = pl.ds(pl.multiple_of(i * 256, 256), 256)
            n, rstd = norm_parts(res[rows, :])
            grad = acc_n[rows, :]
            ggain[...] += jnp.sum(grad * n, axis=0, keepdims=True)
            gshift[...] += jnp.sum(grad, axis=0, keepdims=True)
            resid = di[rows, :].astype(f32) + norm_back(n, rstd, grad, gain[...])
            rg[rows, :] = resid
            low = resid.astype(bf16)
            bg[rows, :] = low
            gb[...] += jnp.sum(low.astype(f32), axis=0, keepdims=True)

    @pl.when(step >= after)
    def _():
        half = bg.shape[1] // 2
        cols = pl.ds(pl.multiple_of((step - after) * half, half), half)
        put_parts(gwu1, dg(oT_scr[...], bg[:, cols], 1, 0), chunks[1], s[1])


def mlp(scalars, devices, cut, oT, x, wo, bo, gain, shift, di, wu, wd, bu, bd):
    total, width = x.shape
    hidden = wu.shape[1]
    rows_block, block = 256, 512
    heads = total // rows_block
    steps = hidden // block
    chunks = hidden // devices, width // devices
    parts = 2 if min(chunks) % 16 == 0 else 1
    down_shape = (width // 2, hidden) if parts == 2 else (hidden, width)
    full = full_spec(total, width)
    vec = full_spec(1, width)

    def early(i):
        return jnp.minimum(i, heads - 1)

    def late(i):
        return jnp.clip(i - heads, 0, steps - 1)

    tokens = pl.BlockSpec((rows_block, width), lambda i, s: (early(i), 0))
    up = pl.BlockSpec((width, block), lambda i, s: (0, late(i)))
    down = pl.BlockSpec((block, width), lambda i, s: (late(i), 0))
    bias = pl.BlockSpec((1, block), lambda i, s: (0, late(i)))
    row = jax.ShapeDtypeStruct((1, width), f32)
    got = call(
        lambda *refs: mlp_kernel(chunks, heads, cut, *refs),
        scalars,
        heads + steps + width // block,
        [oT, x, wo, bo, gain, shift, wu, wd, bu, bd, *di],
        [
            pl.BlockSpec((width, rows_block), lambda i, s: (0, early(i))),
            tokens,
            full_spec(width, width),
            vec,
            vec,
            vec,
            up,
            down,
            bias,
            vec,
        ]
        + [full_spec(rows_block, width)] * heads,
        [jax.ShapeDtypeStruct((rows_block, width), bf16)] * heads
        + [
            jax.ShapeDtypeStruct((1, hidden), f32),
            jax.ShapeDtypeStruct((total, width), f32),
            jax.ShapeDtypeStruct((total, width), bf16),
            row,
            row,
            row,
        ]
        + [jax.ShapeDtypeStruct(down_shape, bf16)] * parts
        + [jax.ShapeDtypeStruct((width // parts, cut * block), bf16)] * parts
        + [jax.ShapeDtypeStruct((width // parts, hidden - cut * block + width), bf16)] * parts,
        [full_spec(rows_block, width)] * heads
        + [bias, full, full, vec, vec, vec]
        + [pl.BlockSpec((down_shape[0] // steps, down_shape[1]), lambda i, s: (late(i), 0))] * parts
        + [
            pl.BlockSpec(
                (width // parts, block), lambda i, s: (0, jnp.clip(i - heads, 0, cut - 1))
            )
        ]
        * parts
        + [
            pl.BlockSpec(
                (width // parts, block), lambda i, s: (0, jnp.maximum(i - heads - cut, 0))
            )
        ]
        * parts,
        [
            pltpu.VMEM((total, width), f32),
            pltpu.VMEM((total, width), f32),
            pltpu.VMEM((total, width), f32),
            pltpu.VMEM((total, width), bf16),
            pltpu.VMEM((total, width), bf16),
            pltpu.VMEM((width, total), bf16),
        ],
        est=cost(2 * total * width * (6 * hidden + 2 * width), 70 * MIB, 2 * total * hidden),
    )
    outs, got = got[:heads], got[heads:]
    return outs, got[:6], got[6 : 6 + parts], got[6 + parts : 6 + 2 * parts], got[6 + 2 * parts :]


def attend_back_kernel(chunk, s, q, k, v, w, bg, oT, olo, aux, g, nT, *refs):
    dqT, dkT, dvT, bias, *grads = refs
    total = k.shape[0]
    row = lax.broadcasted_iota(jnp.int32, (HALF, total), 0)
    codes = g[...]
    qT, kT, vT = q[...].T, k[...].T, v[...].T
    doT = dg(w[...], bg[...], 1, 1).astype(bf16)
    parts = [[], [], []]
    for h in range(2):
        head = slice(h * HALF, (h + 1) * HALF)
        ka = jnp.concatenate([kT[head, :], codes], 0)
        va = jnp.concatenate([vT[head, :], codes], 0)
        doh, qh, ax = doT[head, :], qT[head, :], aux[head, :]
        full = oT[head, :].astype(f32) + olo[head, :].astype(f32)
        delta = -jnp.sum(doh.astype(f32) * full, axis=0, keepdims=True)
        dx = pieces(delta, row, 0.0).astype(bf16)
        qa = jnp.concatenate([qh, ax], 0)
        doa = jnp.concatenate([doh, dx], 0)
        scores = dg(qa, ka, 0, 0)
        dp = dg(doa, va, 0, 0)
        p = jnp.exp(scores)
        low = p.astype(bf16)
        ds = (p * dp).astype(bf16)
        parts[1].append(dg(qh, ds, 1, 0).astype(bf16))
        parts[2].append(dg(doh, low, 1, 0).astype(bf16))
        parts[0].append((dg(kT[head, :], ds, 1, 1) * 0.125).astype(bf16))
    new = jnp.concatenate([p for pair in parts for p in pair], 0)
    for n, ref in enumerate((dqT, dkT, dvT)):
        ref[...] = new[128 * n : 128 * (n + 1)]
    put_parts(grads, dg(nT[...], new, 1, 1), chunk, s[1])
    bias[...] = dg(jnp.ones((8, total), bf16), new, 1, 1)[:1]


def attend_back(scalars, devices, first, pairs, q, k, v, w, bg, oT, olo, aux, g, nT, before):
    total, width = q.shape
    chunk = width // devices
    parts = 2 if chunk % 16 == 0 else 1
    pair = pl.BlockSpec((128, total), lambda i, s: (i + first, 0))
    tall = pl.BlockSpec((total, 128), lambda i, s: (0, i + first))
    done = pl.BlockSpec((128, total), lambda i, s: (i, 0))
    outs = call(
        lambda *refs: attend_back_kernel(chunk, *refs[:11], *refs[11 + len(before) :]),
        scalars,
        pairs,
        [q, k, v, w, bg, oT, olo, aux, g, nT, *before],
        [tall, tall, tall, pl.BlockSpec((128, width), lambda i, s: (i + first, 0))]
        + [full_spec(total, width), pair, pair, pair]
        + [full_spec(HALF, total), full_spec(width, total)]
        + [pl.BlockSpec(memory_space=pl.ANY)] * len(before),
        [jax.ShapeDtypeStruct((128 * pairs, total), bf16)] * 3
        + [jax.ShapeDtypeStruct((1, 384 * pairs), f32)]
        + [jax.ShapeDtypeStruct((width // parts, 3 * width), bf16)] * parts,
        [done] * 3
        + [pl.BlockSpec((1, 384), lambda i, s: (0, i))]
        + [pl.BlockSpec((width // parts, 384), lambda i, s: (0, i + first))] * parts,
        aliases={11 + n: 4 + n for n in range(len(before))},
        est=cost(pairs * 100 * 2 * total * total * 64, pairs * 3 * MIB, pairs * 2 * total * total),
    )
    return outs[:3], outs[3], list(outs[4:])


def token_grad_kernel(count, groups, s, *refs):
    grads = refs[:count]
    wq, wk, wv, x, rg, gain, *more = refs[count:-6]
    outs, eight, acc = refs[-6:-2], refs[-2], refs[-1]
    biases, rows = more[:groups], more[groups:]
    step = pl.program_id(0)

    @pl.when(step == 0)
    def _():
        eight[...] = jnp.zeros_like(eight)
        acc[...] = jnp.zeros_like(acc)
        for n, ref in enumerate(rows):
            eight[4 + n : 5 + n, :] = ref[...]
        at = 0
        for ref in biases:
            for n in range(ref.shape[1] // 384):
                eight[2:3, at : at + 128] = ref[:, 384 * n : 384 * n + 128]
                eight[3:4, at : at + 128] = ref[:, 384 * n + 256 : 384 * n + 384]
                at += 128

    grad = acc[...]
    new = 0.0
    for n, w in enumerate((wq, wk, wv)):
        new = new + dg(jnp.concatenate([g[...] for g in grads[n::3]], 0), w[...], 0, 1)
    n, rstd = norm_parts(x[...].astype(f32))
    eight[0:1, :] += jnp.sum(grad * n, axis=0, keepdims=True)
    eight[1:2, :] += jnp.sum(grad, axis=0, keepdims=True)
    done = (rg[...] + norm_back(n, rstd, grad, gain[...])).astype(bf16)
    for j, out in enumerate(outs):

        @pl.when((step - 1) == (s[2] ^ j))
        def _(out=out):
            out[...] = done

    acc[...] = new


def token_grad(scalars, grads, wq, wk, wv, x, rg, gain, biases, rows):
    total, width = x.shape
    block = 256
    steps = total // block
    grads = [g for triple in grads for g in triple]

    def now(i):
        return jnp.minimum(i, steps - 1)

    def past(i):
        return jnp.maximum(i - 1, 0)

    tokens = pl.BlockSpec((block, width), lambda i, s: (past(i), 0))
    vec = full_spec(1, width)
    return call(
        lambda *refs: token_grad_kernel(len(grads), len(biases), *refs),
        scalars,
        steps + 1,
        [*grads, wq, wk, wv, x, rg, gain, *biases, *rows],
        [pl.BlockSpec((g.shape[0], block), lambda i, s: (0, now(i))) for g in grads]
        + [full_spec(width, width)] * 3
        + [tokens, tokens, vec]
        + [full_spec(*b.shape) for b in biases]
        + [vec] * len(rows),
        [jax.ShapeDtypeStruct((block, width), bf16)] * steps
        + [jax.ShapeDtypeStruct((8, width), f32)],
        [full_spec(block, width)] * steps + [full_spec(8, width)],
        [pltpu.VMEM((block, width), f32)],
        est=cost(6 * total * width * width, 24 * MIB),
    )


def gather_kernel(s, *refs):
    parts, (out, sems) = refs[:-2], refs[-2:]
    copies = [
        pltpu.make_async_copy(ref, out.at[s[2] ^ j], sems.at[j]) for j, ref in enumerate(parts)
    ]
    for copy in copies:
        copy.start()
    for copy in copies:
        copy.wait()


def gather(scalars, parts):
    return call(
        gather_kernel,
        scalars,
        1,
        parts,
        [full_spec(*part.shape) for part in parts],
        jax.ShapeDtypeStruct((len(parts), *parts[0].shape), parts[0].dtype),
        pl.BlockSpec(memory_space=pl.ANY),
        [pltpu.SemaphoreType.DMA((len(parts),))],
    )


AXES = ("rows", "seq")


def swap(values, mask, devices):
    return lax.ppermute(values, AXES, [(d, d ^ mask) for d in range(devices)])


def add_kernel(jobs, arrays, s, *refs):
    many = sum(count_out for _, _, count_out in jobs)
    ins, outs = refs[:arrays], refs[arrays : arrays + many]
    refs = list(refs[arrays + many :])
    sem_in, sem_out = refs[-2:]
    loads, stores, at, count, first_out = [], [], 0, 0, 0
    for job, (free, segments, count_out) in enumerate(jobs):
        result = refs[at : at + count_out]
        at += count_out
        places = []
        for width, terms in segments:
            places.append((width, refs[at : at + len(terms)]))
            at += len(terms)
        for piece in range(2 if free else 1):
            copies = []
            for (width, terms), (_, buffers) in zip(segments, places):
                for buffer, (array, index, column) in zip(buffers, terms):
                    where, first = [], True
                    for entry in index:
                        if entry is None:
                            where.append(piece if first else slice(None))
                            first = False
                        else:
                            where.append(s[entry])
                    where += [slice(None), pl.ds(column, width)]
                    copies.append(
                        pltpu.make_async_copy(
                            ins[array].at[tuple(where)],
                            buffer.at[piece] if free else buffer,
                            sem_in.at[count],
                        )
                    )
                    copies[-1].start()
                    count += 1
            loads.append((outs[first_out : first_out + count_out], piece, free, places, result, copies))
        first_out += count_out
    for targets, piece, free, places, result, copies in loads:
        for copy in copies:
            copy.wait()
        for n in range(2 ** max(free - 1, 0)):
            here = ((piece,) if free else ()) + tuple(n >> b & 1 for b in range(free - 1))
            column = 0
            for width, buffers in places:
                total = sum(buffer[here].astype(f32) for buffer in buffers)
                total = total.astype(result[0].dtype)
                if len(result) == 1:
                    result[0][here + (slice(None), slice(column, column + width))] = total
                else:
                    for block in range(0, width, 128):
                        turn, which = divmod((column + block) // 128, len(result))
                        result[which][:, 128 * turn : 128 * (turn + 1)] = total[:, block : block + 128]
                column += width
        for buffer, target in zip(result, targets):
            stores.append(
                pltpu.make_async_copy(
                    buffer.at[piece] if free else buffer,
                    target.at[piece] if free else target,
                    sem_out.at[len(stores)],
                )
            )
            stores[-1].start()
    for copy in stores:
        copy.wait()


def add_all(table, wanted):
    arrays, jobs, scratch, outs, shapes = [], [], [], [], []
    copies = pieces_out = 0
    for dtype, chunk, free, segments, count_out in wanted:
        shape = (2,) * free + (chunk, sum(width for width, _ in segments) // count_out)
        scratch += [pltpu.VMEM(shape, dtype)] * count_out
        outs += [jax.ShapeDtypeStruct(shape, dtype)] * count_out
        pieces_out += 2 if free else count_out
        listed = []
        for width, terms in segments:
            row = []
            for array, index, column in terms:
                found = [n for n, other in enumerate(arrays) if other is array]
                if not found:
                    arrays.append(array)
                    shapes.append((2,) * len(index) + (chunk, array.shape[-1]))
                row.append((found[0] if found else len(arrays) - 1, index, column))
                scratch.append(pltpu.VMEM((2,) * free + (chunk, width), array.dtype))
                copies += 2 if free else 1
            listed.append((width, row))
        jobs.append((free, listed, count_out))
    anyspec = pl.BlockSpec(memory_space=pl.ANY)
    got = call(
        lambda *refs: add_kernel(jobs, len(arrays), *refs),
        table,
        1,
        [array.reshape(shape) for array, shape in zip(arrays, shapes)],
        [anyspec] * len(arrays),
        outs,
        [anyspec] * len(outs),
        scratch + [pltpu.SemaphoreType.DMA((copies,)), pltpu.SemaphoreType.DMA((pieces_out,))],
    )
    return [values.reshape(-1, values.shape[-1]) for values in got]


class Sum:
    def __init__(self, net, spots, segments, order):
        self.net, self.spots, self.order = net, list(spots), list(order)
        self.devices, self.table = net
        self.sending, self.coming, self.taken, self.total, self.shares = [], [], [], None, 1
        if segments:
            self.chunk = segments[0][0][0].shape[0] >> len(self.spots)
        self.segments = [
            (width, [(array, list(self.spots), column) for array in arrays])
            for arrays, column, width in segments
        ]

    def merged(self, other, order):
        new = Sum(self.net, self.spots, [], order)
        new.chunk, new.taken = self.chunk, list(self.taken)
        new.segments = self.segments + other.segments
        return new

    def wanted(self, mask, dtype, segments):
        nbits = self.devices.bit_length() - 1
        bits = {bit: bit + nbits * (mask >> bit & 1) for bit in self.taken}
        listed = [
            (width, [(v, [bits.get(bit) for bit in spots], column) for v, spots, column in terms])
            for width, terms in segments
        ]
        return (dtype, self.chunk, len(self.spots), listed, self.shares if dtype == f32 else 1)

    def masks(self):
        step = self.order.pop(0)
        bits = step if isinstance(step, tuple) else (step,)
        masks = [0]
        for bit in bits:
            masks += [m | 1 << bit for m in masks]
        self.taken += bits
        for bit in bits:
            self.spots.remove(bit)
        return masks[1:]

    def start(self):
        self.coming += [swap(v, mask, self.devices) for mask, v in self.sending]
        self.sending = []

    def arrive(self, coming):
        column = 0
        for width, terms in self.segments:
            terms += [(v, list(self.spots), column) for v in coming]
            column += width
        self.coming = []


def prepare(sums, more=()):
    jobs = []
    for t in sums:
        if t.order:
            jobs += [(t, mask, bf16, t.segments) for mask in t.masks()]
        elif t.total is None:
            whole = [t.segments] if t.shares > 1 else [[segment] for segment in t.segments]
            jobs += [(t, 0, f32, segments) for segments in whole]
            t.total = []
    if not jobs and not more:
        return []
    got = add_all(sums[0].table, [t.wanted(mask, dtype, segments) for t, mask, dtype, segments in jobs] + list(more))
    for t, mask, dtype, _ in jobs:
        if dtype == f32:
            t.total += got[: t.shares]
            got = got[t.shares :]
        else:
            t.sending.append((mask, got[0]))
            got = got[1:]
    return got


def together(*groups):
    flat = lax.optimization_barrier(tuple(v for group in groups for v in group))
    out, start = [], 0
    for group in groups:
        out.append(list(flat[start : start + len(group)]))
        start += len(group)
    return out


def arrive(sums, carry):
    got = together(carry, *[t.coming for t in sums])
    for t, coming in zip(sums, got[1:]):
        t.arrive(coming)
    return got[0]


def leave(sums, carry):
    prepare(sums)
    got = together(carry, *[[v for _, v in t.sending] for t in sums])
    for t, sending in zip(sums, got[1:]):
        t.sending = [(mask, v) for (mask, _), v in zip(t.sending, sending)]
        t.start()
    return got[0]


def on_device(
    tokens,
    segment_ids,
    grad_out,
    norm1_gain,
    norm1_shift,
    w_query,
    b_query,
    w_key,
    w_value,
    b_value,
    w_out,
    b_out,
    norm2_gain,
    norm2_shift,
    w_up,
    b_up,
    w_down,
    b_down,
):
    row_count, local_len, width = tokens.shape
    full_len = segment_ids.shape[1]
    hidden = w_up.shape[1]
    seq, rows = lax.axis_size("seq"), lax.axis_size("rows")
    devices = rows * seq
    me = lax.axis_index("seq")
    core, pair = me % 2, me // 2
    assert row_count == seq == 4 and local_len * seq == full_len

    def vec(v):
        return v.reshape(1, -1)

    def scalars(first):
        return jnp.stack([jnp.int32(first), jnp.int32(core), jnp.int32(me)])

    def exchange(parts):
        return [parts[0]] + [swap(parts[j], j, devices) for j in range(1, seq)]

    plain = scalars(0)
    def pick(values, j):
        return lax.dynamic_index_in_dim(values, me ^ j, 0, keepdims=False)

    distant = [pick(tokens, j) for j in (2, 3)]
    distant, [near] = together(distant, [tokens])
    chunks = exchange([pick(near, 0), pick(near, 1), *distant])
    norm1 = (vec(norm1_gain), vec(norm1_shift))
    weights = (w_query, w_key, w_value, vec(b_query), vec(b_value))

    ids = lax.dynamic_index_in_dim(segment_ids, me, 0, keepdims=False)
    digits = jnp.stack([(ids // BASE**n) % BASE for n in range(DIGITS)], 1)
    hot = (digits[:, :, None] == jnp.arange(BASE)[None, None, :]).reshape(full_len, CODE)
    hot = hot.astype(f32)
    rest = jnp.zeros((full_len, HALF - CODE), f32)
    query_code = jnp.concatenate([hot, rest], 1).astype(bf16).T
    key_code = jnp.concatenate([-1e30 * (1.0 - hot), rest.at[:, :3].set(1.0)], 1).astype(bf16)
    key_codeT = key_code.T
    key_code = jnp.concatenate([key_code, key_code], 1)

    local_ids = lax.dynamic_slice_in_dim(segment_ids, me * local_len, local_len, 1)
    is_image = (local_ids != full_len).astype(bf16)[:, :, None]
    out_grad = grad_out * is_image
    grad_b_down = jnp.sum(out_grad.astype(f32), axis=(0, 1))

    before = qkv(scalars(pair), chunks[:2], *norm1, *weights, ())
    before = list(before)
    [before[0]], [out_grad] = together([before[0]], [out_grad])
    others = chunks[2:]
    down_in = exchange([pick(out_grad, j) for j in range(seq)])
    x, normedT, q, k, v = qkv(scalars(1 - pair), others, *norm1, *weights, before)
    oT, olo, aux = attend(q, k, v, query_code, key_code)
    nbits = devices.bit_length() - 1
    far = tuple(range(3, nbits))
    every = list(range(nbits - 1, -1, -1))
    block_out, (grad_b_up, rg, bg, gain2, shift2, bias_out), grad_down, grad_up0, grad_up1 = mlp(
        plain,
        devices,
        4,
        oT,
        x,
        w_out,
        vec(b_out),
        vec(norm2_gain),
        vec(norm2_shift),
        down_in,
        w_up,
        w_down,
        vec(b_up),
        vec(b_down),
    )
    biases, grads = [], []

    def backward(first, pairs, bg, before):
        got, bias, parts = attend_back(
            plain, devices, first, pairs, q, k, v, w_out, bg, oT, olo, aux, key_codeT, normedT, before
        )
        grads.append(got)
        biases.append(bias)
        return parts

    split = len(grad_down) == 2 and nbits == 5
    own_bits = [lax.axis_index(AXES) >> n & 1 for n in range(nbits)]
    table = jnp.stack([jnp.int32(n) for n in (*own_bits, *(1 - n for n in own_bits), 0, 1)])
    net = devices, table
    spots = every[:-1]

    def on_chip(pairs, carry):
        sends = [pair_[0] for pair_ in pairs]
        carry, sends = together(carry, sends)
        return carry, [swap(v, 1, devices) for v in sends]

    made = [grad_down, grad_up0, grad_up1]
    block_out = list(block_out)
    if split:
        [bg], came = on_chip(made, [bg])
    block_out[2:] = [swap(block_out[j], j, devices) for j in range(2, seq)]
    parts = backward(0, 2, bg, ())
    if split:
        (parts[0], bg, *block_out[2:]), came = together([parts[0], bg, *block_out[2:]], came)
        down, up0, up1 = ([keep, other] for (_, keep), other in zip(made, came))
        sum_a = Sum(net, spots, [(down, 0, 3328)], [2, 1])
        sum_b = Sum(net, spots, [(down, 3328, 768), (up1, 512, 2560)], [1, 2])
        sum_c = Sum(net, spots, [(up0, 0, 2048), (up1, 0, 512)], [3, 4, 1, 2])
        sums = [sum_a, sum_b, sum_c]
        parts[0], bg = leave(sums, [parts[0], bg])
    block_out[1] = swap(block_out[1], 1, devices)
    parts = backward(2, 4, bg, parts)
    if split:
        parts[0], bg, *block_out = arrive(sums, [parts[0], bg, *block_out])
        parts[0], bg = leave(sums, [parts[0], bg])
    block_out = gather(plain, block_out)
    parts = backward(6, 2, bg, parts)
    gain = vec(norm1_gain)
    if split:
        parts[0], gain, block_out = arrive(sums, [parts[0], gain, block_out])
        [gain], came = on_chip([parts], [gain])
        sum_ab = sum_a.merged(sum_b, [3, 4])
        sums = [sum_ab, sum_c]
        [gain] = leave(sums, [gain])
        [gain], came = together([gain], came)
        ours = [parts[1], *came]
        cols = parts[1].shape[1] // 2
        sum_d = Sum(net, spots, [(ours, 0, cols)], [2, 1])
        sum_e = Sum(net, spots, [(ours, cols, cols)], [1, 2])
        [gain] = leave([sum_d, sum_e], [gain])
        sums += [sum_d, sum_e]
    *token, eight = token_grad(
        plain,
        grads,
        w_query,
        w_key,
        w_value,
        x,
        rg,
        gain,
        biases,
        [bias_out, gain2, shift2, vec(grad_b_down)],
    )
    own = width // devices
    eight = jnp.transpose(eight.reshape(8, devices, -1), (1, 0, 2)).reshape(devices, -1)
    vectors = jnp.concatenate([eight, grad_b_up.reshape(devices, -1)], 1)
    if split:
        token = arrive(sums, token)
        token = leave(sums, token)
        token[2] = swap(token[2], 2, devices)
        token = arrive([sum_ab, sum_c, sum_d, sum_e], token)
        both = sum_d.merged(sum_e, [])
        [blocks] = prepare([sum_ab, sum_c], [both.wanted(0, bf16, both.segments)])
        token, [blocks] = together(token, [blocks])
        along = [[d for d in range(devices) if d % 8 == low] for low in range(8)]
        blocks = lax.all_to_all(blocks, AXES, 0, 0, axis_index_groups=along, tiled=True)
    else:
        token[2] = swap(token[2], 2, devices)
    vectors = lax.all_to_all(vectors, AXES, 0, 0, tiled=True)
    token[1], token[3] = swap(token[1], 1, devices), swap(token[3], 3, devices)
    if split:
        width_in = blocks.shape[1]
        zero = 2 * nbits
        terms = [(blocks, [zero + place // 2, zero + place % 2], 0) for place in range(4)]
        grad_w_query, grad_w_key, grad_w_value = add_all(
            table, [(f32, both.chunk, 0, [(width_in, terms)], 3)]
        )
        down0, down1, up1 = sum_ab.total
        up0, up_mid = sum_c.total
        grad_w_down = jnp.concatenate([down0, down1], 1).reshape(own, -1, width)
        grad_w_down = jnp.transpose(grad_w_down, (1, 0, 2)).reshape(-1, width)
        at = up1.shape[1] - width
        grad_w_up = jnp.concatenate([up0, up_mid, up1[:, :at]], 1)
        grad_w_out = up1[:, at:]
    else:

        def over_all(values):
            return lax.psum_scatter(values.astype(f32), AXES, scatter_dimension=0, tiled=True)

        grad_w_down, up0, up1, qkv_sums = (over_all(pair_[0]) for pair_ in (*made, parts))
        qkv_sums = qkv_sums.reshape(own, width // 128, 3, 128)
        grad_w_query, grad_w_key, grad_w_value = (
            qkv_sums[:, :, n].reshape(own, width) for n in range(3)
        )
        grad_w_up = jnp.concatenate([up0, up1[:, : hidden - up0.shape[1]]], 1)
        grad_w_out = up1[:, hidden - up0.shape[1] :]
    vectors = jnp.sum(vectors, 0)
    grad_tokens = gather(plain, token)
    parts, start = [], 0
    for size in [width] * 8 + [hidden]:
        parts.append(vectors[start : start + size // devices])
        start += size // devices
    gain1, shift1, bq, bv, bo, gain2, shift2, bd, bu = parts
    return (
        block_out,
        grad_tokens,
        gain1,
        shift1,
        grad_w_query,
        bq,
        grad_w_key,
        grad_w_value,
        bv,
        grad_w_out,
        bo,
        gain2,
        shift2,
        grad_w_up,
        bu,
        grad_w_down,
        bd,
    )


def solution(mesh):
    tokens = P("rows", "seq", None)
    spread = P(("rows", "seq"))
    spread2 = P(("rows", "seq"), None)
    return jax.shard_map(
        on_device,
        mesh=mesh,
        in_specs=(tokens, P("rows", None), tokens) + (P(),) * 15,
        out_specs=(
            tokens,
            tokens,
            spread,
            spread,
            spread2,
            spread,
            spread2,
            spread2,
            spread,
            spread2,
            spread,
            spread,
            spread,
            spread2,
            spread,
            spread2,
            spread,
        ),
        check_vma=False,
    )
```
